512 devices in a mesh: seq: 64 (over y, z), mp: 8 (over x, core).
Axes of the slice: x: 4, y: 4, z: 16, core: 2. Of those that a mesh axis runs over, the one named last changes fastest.
Arguments:
- projections: bfloat16 [16384, 6144], P('seq', 'mp'), may hold values from -80 to 80
- qk_gain: float32 [2, 128], replicated, may hold values from 0.1 to 1.9
- clusters: int32 [16, 16384, 1], P('mp', 'seq'), may hold values from 0 to 63; in each aligned block of 256 rows (0 to 255, 256 to 511, ..., all dimensions but the last counted through in order) at most 10 rows name the same one
- d_out: bfloat16 [16384, 4096], P('seq'), may hold values from -64 to 64
- w_out: bfloat16 [4096, 2048], P(None, 'mp'), may hold values from -0.125 to 0.125
Outputs:
- d_projections: bfloat16 [16384, 6144], P('seq', 'mp')
- d_w_out: float32 [4096, 2048], P('seq', 'mp')
The draws below stay inside these ranges and needn't reach their ends.
Inputs may be any that keep to these rules, and one draw needn't show every extreme that they name: `clusters`: for each head, among the 256 tokens of one index of seq no cluster holds more than 10 tokens, and some cluster holds exactly 10 of them for some head and index.
All inputs are finite; a program needn't handle non-finite values.
Results may differ from the reference program's by a relative error of at most 0.009.
Values may be sent and summed in bfloat16 or wider, within the bound.
A program may use at most 64 MiB of HBM per device.

```python
import math
import jax
import jax.numpy as jnp
import numpy as np
from jax import lax

D = 4096
HEADS = 16
HS = 128
TOK_DEV = 256
TOKENS = 16384
CLUSTERS = 64
CAP = 10
SLOTS = 640


def draw_projections(key, part):
    key = jax.random.fold_in(key, 7)
    first, second = jax.random.split(key, 2)
    width = HEADS * 3 * HS
    spread = jnp.exp(jax.random.uniform(second, (1, width), jnp.float32, 0.0, math.log(10.0))) / 3.0
    drawn = jax.random.normal(first, (TOKENS, width), jnp.float32)
    return (drawn * spread).astype(jnp.bfloat16)


def raised(array, rng, source, target, parts, factor):
    def block_of(position):
        return (jnp.arange(array.shape[position]) // (array.shape[position] // parts)).reshape((-1,) + (1,) * (array.ndim - 1 - position))

    first = jax.random.permutation(rng, parts)[block_of(target)]
    other_side = (block_of(target) + parts // 2) % parts
    return jnp.where((block_of(source) == first) | (block_of(source) == other_side), factor * array, array)


def steps_of(key, extent, cuts, low, high):
    factor_of, own = 1.0, jax.random.fold_in(key, 6)
    for axis_at, parts in cuts:
        heights = jnp.exp(jax.random.uniform(jax.random.fold_in(own, axis_at), (parts,), jnp.float32, low / len(cuts), high / len(cuts)))
        factor_of = factor_of * jnp.repeat(heights, extent[axis_at] // parts).reshape([-1 if axis == axis_at else 1 for axis in range(len(extent))])
    return factor_of


def routed_block(key, own, number, rows, count, top, bound, skew):
    sequence = jax.random.permutation(key, count)
    packed, ordinary = shares(count, rows * top, bound, skew, True), shares(count, rows * top, bound, skew, False)
    places = jnp.arange(count)

    def named(tallies, turn):
        used = int((tallies > 0).sum())
        fixed = max(1, used // 4)
        shifted = fixed + (places - fixed + turn * (used - fixed)) % max(1, count - fixed)
        return jnp.zeros((count,), jnp.int32).at[sequence[jnp.where(places < fixed, places, shifted)]].set(jnp.asarray(tallies, jnp.int32))

    tallies = jnp.where(number % 4 == 0, named(packed, number // 4), named(ordinary, number - number // 4 - 1))
    mixed = jax.random.permutation(jax.random.fold_in(own, 3), count)
    giver, taker = mixed[0:count // 2 * 2:2], mixed[1:count // 2 * 2:2]
    margin = jnp.minimum(tallies[giver] - 1, bound - tallies[taker]) // 2
    margin = jnp.where((giver == sequence[0]) | (taker == sequence[0]) | (tallies[taker] == 0), 0, jnp.maximum(margin, 0))
    shifted = jax.random.randint(jax.random.fold_in(own, 4), (count // 2,), 0, 1 << 20) % (margin + 1)
    tallies = tallies.at[giver].add(-shifted).at[taker].add(shifted)
    items = jnp.searchsorted(jnp.cumsum(tallies), jnp.arange(rows * top), side="right").astype(jnp.int32)
    listing = items.reshape(top, rows).T
    listing = listing[jax.random.permutation(jax.random.fold_in(own, 1), rows)]
    turn = jax.random.randint(jax.random.fold_in(own, 2), (rows, 1), 0, top)
    return jnp.take_along_axis(listing, (jnp.arange(top)[None, :] + turn) % top, axis=1)


def shares(number_of, total, reach, lean, full):
    weights = [(1 << 20) // math.isqrt(rank ** lean) + 1 for rank in range(1, number_of + 1)]
    largest = reach if full else min(reach, max(-(-total // number_of), total * weights[0] // sum(weights)))
    least = 1 if total - largest >= number_of - 1 else 0
    given, rest = [largest] + [least] * (number_of - 1), total - largest - least * (number_of - 1)
    while rest > 0:
        free = [i for i in range(1, number_of) if given[i] < largest] or [i for i in range(1, number_of) if given[i] < reach]
        whole, remaining = sum([weights[i] for i in free]), rest
        for i in free:
            extra = min(reach - given[i], max(1, remaining * weights[i] // whole), rest)
            given[i] = given[i] + extra
            rest = rest - extra
    return np.array(given)


def gaussian(rng, shape, scale, most, pieces=(), held_as=jnp.bfloat16):
    entries = jax.random.normal(rng, shape, jnp.float32) * scale
    if len(pieces) > 0:
        entries = steps_of(rng, shape, pieces, -0.22, 0.18) * entries
    return jnp.clip(entries, min=-most, max=most).astype(held_as)


def gaussian_with(key, shape, scale, limit, cuts, heavy, dtype=jnp.bfloat16):
    values = scale * jax.random.normal(key, shape, jnp.float32)
    if cuts:
        values = values * steps_of(key, shape, cuts, -0.22, 0.18)
    return jnp.clip(raised(values, jax.random.fold_in(key, 3), *heavy), -limit, limit).astype(dtype)


def setup_inputs(seed: int = 0) -> dict:
    arg_keys = jax.random.split(jax.random.key(seed), 6)
    projections = draw_projections(jax.random.fold_in(arg_keys[5], 71), 0)
    qk_gain = jnp.clip(1.0 + 0.18 * jax.random.normal(arg_keys[1], (2, HS), jnp.float32), 0.1, 1.9)
    clusters_keys = jax.random.split(jax.random.fold_in(arg_keys[2], 1), HEADS * TOKENS // TOK_DEV)
    clusters_turns = jax.random.permutation(jax.random.fold_in(arg_keys[2], 3), HEADS * TOKENS // TOK_DEV)
    clusters = jax.vmap(lambda own, number: routed_block(jax.random.fold_in(arg_keys[2], 2), own, number, TOK_DEV, CLUSTERS, 1, CAP, 2))(clusters_keys, clusters_turns).reshape((HEADS, TOKENS, 1))
    d_out = gaussian_with(arg_keys[3], (TOKENS, D), 4.0, 64.0, ((0, 64),), (0, 1, 64, 4.0))
    w_out = gaussian(arg_keys[4], (D, HEADS * HS), (HEADS * HS) ** -0.5, 0.125, ((1, 8),))
    return {"projections": projections, "qk_gain": qk_gain, "clusters": clusters, "d_out": d_out, "w_out": w_out}


EPSILON = 1e-06

def normalize(raw):
    data = raw.astype(jnp.float32)
    inverse = lax.rsqrt(lax.optimization_barrier(jnp.mean(data * data, axis=-1, keepdims=True)) + EPSILON)
    return (data * inverse, inverse)

def norm_back(unit, inverse, gain, upstream):
    scaled = upstream * gain
    return inverse * (scaled - unit * lax.optimization_barrier(jnp.mean(scaled * unit, axis=-1, keepdims=True)))

def attend_block(query_hat, key_hat, values, grad_out, live):
    scale = HS ** (-0.5)
    scores = jnp.dot(query_hat, key_hat.T, preferred_element_type=jnp.float32) * scale
    expo = jnp.exp(scores) * live[None, :]
    denominator = lax.optimization_barrier(jnp.sum(expo, axis=-1, keepdims=True)) + (1.0 - live)[:, None]
    probs = expo / denominator
    probs_low = probs.astype(jnp.bfloat16)
    output = jnp.dot(probs_low, values, preferred_element_type=jnp.float32)
    grad_probs = jnp.dot(grad_out, values.T, preferred_element_type=jnp.float32)
    row_dot = lax.optimization_barrier(jnp.sum(probs * grad_probs, axis=-1, keepdims=True))
    grad_scores = (probs * (grad_probs - row_dot) * scale).astype(jnp.bfloat16)
    grad_query = jnp.dot(grad_scores, key_hat, preferred_element_type=jnp.float32)
    grad_key = jnp.dot(grad_scores.T, query_hat, preferred_element_type=jnp.float32)
    grad_value = jnp.dot(probs_low.T, grad_out, preferred_element_type=jnp.float32)
    return jnp.concatenate([output, grad_query, grad_key, grad_value], axis=-1).astype(jnp.bfloat16)

def reference(projections, qk_gain, clusters, d_out, w_out):
    split_proj = projections.reshape(TOKENS, HEADS, 3, HS)
    query_unit, query_inverse = normalize(split_proj[:, :, 0])
    key_unit, key_inverse = normalize(split_proj[:, :, 1])
    query_hat = (query_unit * qk_gain[0]).astype(jnp.bfloat16)
    key_hat = (key_unit * qk_gain[1]).astype(jnp.bfloat16)
    values = split_proj[:, :, 2]
    grad_attention = jnp.dot(d_out, w_out, preferred_element_type=jnp.float32).astype(jnp.bfloat16)
    grad_attention = grad_attention.reshape(TOKENS, HEADS, HS)
    ident = clusters[:, :, 0]

    def per_head(bundle):
        head_query, head_key, head_value, head_grad, head_ids = bundle

        def per_cluster(cluster):
            member = head_ids == cluster
            places = jnp.nonzero(member, size=SLOTS, fill_value=0)[0]
            number = jnp.sum(member.astype(jnp.int32))
            live = (jnp.arange(SLOTS) < number).astype(jnp.float32)
            live_low = live.astype(jnp.bfloat16)[:, None]
            result = attend_block(head_query[places] * live_low, head_key[places] * live_low, head_value[places] * live_low, head_grad[places] * live_low, live)
            return (places, result.astype(jnp.float32) * live[:, None])
        places, results = lax.map(per_cluster, jnp.arange(CLUSTERS))
        filled = jnp.zeros((TOKENS, 4 * HS), jnp.float32).at[places.reshape(-1)].add(results.reshape(-1, 4 * HS))
        return filled.astype(jnp.bfloat16)
    bundles = (query_hat.transpose(1, 0, 2), key_hat.transpose(1, 0, 2), values.transpose(1, 0, 2), grad_attention.transpose(1, 0, 2), ident)
    gathered = lax.map(per_head, bundles).transpose(1, 0, 2).astype(jnp.float32)
    attention = gathered[:, :, :HS].astype(jnp.bfloat16).reshape(TOKENS, HEADS * HS)
    grad_query = norm_back(query_unit, query_inverse, qk_gain[0], gathered[:, :, HS:2 * HS])
    grad_key = norm_back(key_unit, key_inverse, qk_gain[1], gathered[:, :, 2 * HS:3 * HS])
    grad_value = gathered[:, :, 3 * HS:]
    d_projections = jnp.stack([grad_query, grad_key, grad_value], axis=2).astype(jnp.bfloat16)
    d_projections = d_projections.reshape(TOKENS, HEADS * 3 * HS)
    d_w_out = jnp.dot(d_out.T, attention, preferred_element_type=jnp.float32) * TOKENS ** (-0.5)
    return (d_projections, d_w_out)
```

```python
import functools

import jax
import jax.numpy as jnp
from jax import lax
from jax.experimental import pallas as pl
from jax.experimental.pallas import tpu as pltpu
from jax.sharding import PartitionSpec as P

EPSILON = 1e-06
HS = 128
HEADS = 2
CAP = 10
MAIN = 8
DEAD = 1024.0
TILE = 16
F32 = jnp.float32
BF16 = jnp.bfloat16

MAIN_ROW = (0, 32, 48, 64)
REST_ROW = 16
ROWS = 80
FIRST = 32


def dot(a, b, dims):
    return lax.dot_general(a, b, (dims, ((), ())), preferred_element_type=F32)


def normalize(raw):
    data = raw.astype(F32)
    inverse = lax.rsqrt(jnp.mean(data * data, axis=-1, keepdims=True) + EPSILON)
    return data * inverse, inverse


def norm_back(unit, inverse, gain, upstream):
    scaled = upstream * gain
    return inverse * (scaled - unit * jnp.mean(scaled * unit, axis=-1, keepdims=True))


def kernel(ny, nz, proj, gain, ids_row, ids_col, d_out, w_out, d_proj, d_w,
           sent, arrived, back1, back2, home1, home2, rest, d_cols, d_cols_t,
           att, att_all, part, part_all, qs, ks, vs, gs, low, grad_low,
           chooser_t, sems):
    n = ny * nz
    tokens = proj.shape[0]
    slots = n * CAP
    width = d_out.shape[1] // ny
    me = lax.axis_index("seq")
    my_y, my_z = me // nz, me % nz

    def other(step):
        j, dy = step // ny, step % ny
        dz = jnp.where(j % 2 == 1, (j + 1) // 2, nz - j // 2)
        return ((my_y + dy) % ny) * nz + (my_z + dz) % nz

    def remote(src, dst, number, target):
        return pltpu.make_async_remote_copy(
            src_ref=src, dst_ref=dst, send_sem=sems.at[2 * number],
            recv_sem=sems.at[2 * number + 1], device_id={"seq": target},
            device_id_type=pl.DeviceIdType.MESH)

    def wait_sent(ref, number):
        pltpu.make_async_copy(ref, ref, sems.at[2 * number]).wait()

    def wait_arrived(ref, number):
        pltpu.make_async_copy(ref, ref, sems.at[2 * number + 1]).wait()

    barrier = pltpu.get_barrier_semaphore()

    @pl.loop(1, n)
    def _(step):
        pl.semaphore_signal(barrier, inc=1, device_id={"seq": other(step)},
                            device_id_type=pl.DeviceIdType.MESH)

    grad_att = dot(d_out[...], w_out[...], ((1,), (0,))).astype(BF16)
    ones = jnp.ones((tokens, HS), BF16)
    packed = []
    for h in range(HEADS):
        first = h * 3 * HS
        q_unit, _ = normalize(proj[:, first:first + HS])
        k_unit, _ = normalize(proj[:, first + HS:first + 2 * HS])
        payload = jnp.concatenate(
            [(q_unit * gain[0:1, :]).astype(BF16), (k_unit * gain[1:2, :]).astype(BF16),
             proj[:, first + 2 * HS:first + 3 * HS], grad_att[:, h * HS:(h + 1) * HS], ones], axis=1)
        row, col = ids_row[h], ids_col[h]
        same = row == col
        t0 = lax.broadcasted_iota(jnp.int32, (tokens, tokens), 0)
        t1 = lax.broadcasted_iota(jnp.int32, (tokens, tokens), 1)
        rank_row = jnp.sum(jnp.where(same & (t0 < t1), 1.0, 0.0), axis=0, keepdims=True).astype(jnp.int32)
        rank_col = jnp.sum(jnp.where(same & (t1 < t0), 1.0, 0.0), axis=1, keepdims=True).astype(jnp.int32)

        def place(ids, rank):
            return jnp.where(rank < MAIN, ids * MAIN + rank, n * MAIN + (rank - MAIN) * n + ids)

        chooser = jnp.where(
            place(row, rank_row) == lax.broadcasted_iota(jnp.int32, (slots, tokens), 0), 1.0, 0.0).astype(BF16)
        chooser_t[h] = jnp.where(
            place(col, rank_col) == lax.broadcasted_iota(jnp.int32, (tokens, slots), 1), 1.0, 0.0).astype(BF16)
        rows = dot(chooser, payload, ((1,), (0,)))
        live = rows[:, 4 * HS:]
        packed.append([rows[:, :HS], rows[:, HS:2 * HS],
                       rows[:, 2 * HS:3 * HS] + (1.0 - live) * DEAD, rows[:, 3 * HS:4 * HS]])

    def main_tile(parts, c):
        both = [parts[h][c][:n * MAIN].reshape(n, MAIN, HS) for h in range(HEADS)]
        return jnp.concatenate(both, axis=1).astype(BF16)

    def rest_tile(parts):
        for h in range(HEADS):
            for c in range(4):
                for r in range(CAP - MAIN):
                    start = n * (MAIN + r)
                    rest[pl.ds(c * 4 + h * 2 + r, n, stride=TILE), :] = parts[h][c][start:start + n]
        return rest[...].reshape(n, TILE, HS).astype(BF16)

    def slots_of(main, c, h):
        pieces = [main.astype(F32)[:, h * MAIN:(h + 1) * MAIN].reshape(n * MAIN, HS)]
        for r in range(CAP - MAIN):
            pieces.append(rest[pl.ds(c * 4 + h * 2 + r, n, stride=TILE), :])
        return jnp.concatenate(pieces, axis=0)

    for c in range(4):
        sent[:, MAIN_ROW[c]:MAIN_ROW[c] + TILE] = main_tile(packed, c)
    sent[:, REST_ROW:REST_ROW + TILE] = rest_tile(packed)

    pl.semaphore_wait(barrier, n - 1)

    @pl.loop(1, n)
    def _(step):
        target = other(step)
        remote(sent.at[target], arrived.at[me], 0, target).start()

    for dy in range(1, ny):
        to_y = (my_y + dy) % ny
        start = pl.multiple_of(to_y * width, width)
        remote(d_out.at[:, pl.ds(start, width)], d_cols.at[my_y], 1, to_y * nz + my_z).start()
    own = pl.multiple_of(my_y * width, width)
    d_cols[my_y] = d_out[:, pl.ds(own, width)]
    arrived[me] = sent[me]

    wait_arrived(arrived.at[pl.ds(0, n - 1)], 0)

    rest[...] = arrived[:, REST_ROW:REST_ROW + TILE].astype(F32).reshape(n * TILE, HS)
    scale = HS ** -0.5
    results = []
    for h in range(HEADS):
        for c, ref in enumerate((qs, ks, vs, gs)):
            rows = slots_of(arrived[:, MAIN_ROW[c]:MAIN_ROW[c] + TILE], c, h)
            if c == 2:
                live = jnp.where(rows < DEAD / 2, 1.0, 0.0)[:, 0:1]
                rows = jnp.where(rows < DEAD / 2, rows, 0.0)
            ref[...] = rows.astype(BF16)
        out_t, grad_q_t = [], []
        for start in range(0, slots, 2 * HS):
            size = min(2 * HS, slots - start)
            block = slice(start, start + size)
            scores = dot(ks[...], qs[block], ((1,), (1,))) * scale
            expo = jnp.exp(scores) * live
            total = jnp.sum(expo, axis=0, keepdims=True)
            total = jnp.where(total == 0.0, 1.0, total)
            probs = expo / total
            probs_low = probs.astype(BF16)
            grad_probs = dot(vs[...], gs[block], ((1,), (1,)))
            row_dot = jnp.sum(probs * grad_probs, axis=0, keepdims=True)
            grad_scores = (probs * (grad_probs - row_dot) * scale).astype(BF16)
            low[:, block] = probs_low
            grad_low[:, block] = grad_scores
            out_t.append(dot(vs[...], probs_low, ((0,), (0,))))
            grad_q_t.append(dot(ks[...], grad_scores, ((0,), (0,))))
        out = jnp.concatenate(out_t, axis=1).T
        grad_q = jnp.concatenate(grad_q_t, axis=1).T
        grad_k = dot(grad_low[...], qs[...], ((1,), (0,)))
        grad_v = dot(low[...], gs[...], ((1,), (0,)))
        results.append([out, grad_q, grad_k, grad_v])
    back1[:, REST_ROW:REST_ROW + TILE] = rest_tile(results)
    back1[:, 0:TILE] = main_tile(results, 0)
    for c in range(1, 4):
        start = MAIN_ROW[c] - FIRST
        back2[:, start:start + TILE] = main_tile(results, c)

    @pl.loop(1, n)
    def _(step):
        target = other(step)
        remote(back1.at[target], home1.at[me], 2, target).start()

    @pl.loop(1, n)
    def _(step):
        target = other(step)
        remote(back2.at[target], home2.at[me], 3, target).start()

    home1[me] = back1[me]
    home2[me] = back2[me]

    wait_arrived(d_cols.at[pl.ds(0, ny - 1)], 1)
    for y in range(ny):
        d_cols_t[:, y * tokens:(y + 1) * tokens] = d_cols[y].T

    wait_arrived(home1.at[pl.ds(0, n - 1)], 2)
    rest[...] = home1[:, REST_ROW:REST_ROW + TILE].astype(F32).reshape(n * TILE, HS)
    for h in range(HEADS):
        rows = slots_of(home1[:, 0:TILE], 0, h).astype(BF16)
        att[:, h * HS:(h + 1) * HS] = dot(chooser_t[h], rows, ((1,), (0,))).astype(BF16)
    for dy in range(1, ny):
        to_y = (my_y + dy) % ny
        remote(att, att_all.at[my_y], 4, to_y * nz + my_z).start()
    att_all[my_y] = att[...]
    wait_arrived(att_all.at[pl.ds(0, ny - 1)], 4)
    gathered = att_all[...].reshape(ny * tokens, HEADS * HS)
    rows_z = width // nz
    part[...] = dot(d_cols_t[...], gathered, ((1,), (0,))).astype(BF16).reshape(nz, rows_z, HEADS * HS)

    @pl.loop(1, nz)
    def _(step):
        to_z = (my_z + jnp.where(step % 2 == 1, (step + 1) // 2, nz - step // 2)) % nz
        remote(part.at[to_z], part_all.at[my_z], 5, my_y * nz + to_z).start()

    part_all[my_z] = part[my_z]

    wait_arrived(home2.at[pl.ds(0, n - 1)], 3)
    for h in range(HEADS):
        grads = []
        for c in range(1, 4):
            start = MAIN_ROW[c] - FIRST
            grads.append(slots_of(home2[:, start:start + TILE], c, h).astype(BF16))
        found = dot(chooser_t[h], jnp.concatenate(grads, axis=1), ((1,), (0,)))
        first = h * 3 * HS
        for c in range(2):
            unit, inverse = normalize(proj[:, first + c * HS:first + (c + 1) * HS])
            d_proj[:, first + c * HS:first + (c + 1) * HS] = norm_back(
                unit, inverse, gain[c:c + 1, :], found[:, c * HS:(c + 1) * HS]).astype(BF16)
        d_proj[:, first + 2 * HS:first + 3 * HS] = found[:, 2 * HS:].astype(BF16)

    wait_arrived(part_all.at[pl.ds(0, nz - 1)], 5)
    total = part_all[0].astype(F32)
    for z in range(1, nz):
        total = total + part_all[z].astype(F32)
    d_w[...] = total * (tokens * n) ** -0.5

    wait_sent(sent.at[pl.ds(0, n - 1)], 0)
    wait_sent(d_cols.at[pl.ds(0, ny - 1)], 1)
    wait_sent(back1.at[pl.ds(0, n - 1)], 2)
    wait_sent(back2.at[pl.ds(0, n - 1)], 3)
    wait_sent(att_all.at[pl.ds(0, ny - 1)], 4)
    wait_sent(part.at[pl.ds(0, nz - 1)], 5)


def per_device(ny, projections, qk_gain, clusters, d_out, w_out):
    tokens = projections.shape[0]
    n = lax.axis_size("seq")
    nz = n // ny
    slots = n * CAP
    width = d_out.shape[1] // ny
    columns = HEADS * HS
    vmem = pltpu.VMEM
    scratch = [
        vmem((n, ROWS, HS), BF16), vmem((n, ROWS, HS), BF16),
        vmem((n, FIRST, HS), BF16), vmem((n, ROWS - FIRST, HS), BF16),
        vmem((n, FIRST, HS), BF16), vmem((n, ROWS - FIRST, HS), BF16),
        vmem((n * TILE, HS), F32),
        vmem((ny, tokens, width), BF16), vmem((width, ny * tokens), BF16),
        vmem((tokens, columns), BF16), vmem((ny, tokens, columns), BF16),
        vmem((nz, width // nz, columns), BF16), vmem((nz, width // nz, columns), BF16),
        vmem((slots, HS), BF16), vmem((slots, HS), BF16), vmem((slots, HS), BF16), vmem((slots, HS), BF16),
        vmem((slots, slots), BF16), vmem((slots, slots), BF16),
        vmem((HEADS, tokens, slots), BF16),
        pltpu.SemaphoreType.DMA((12,)),
    ]
    whole = pl.BlockSpec(memory_space=pltpu.VMEM)
    return pl.pallas_call(
        functools.partial(kernel, ny, nz),
        out_shape=(jax.ShapeDtypeStruct(projections.shape, BF16),
                   jax.ShapeDtypeStruct((width // nz, columns), F32)),
        in_specs=[whole] * 6,
        out_specs=(whole, whole),
        scratch_shapes=scratch,
        compiler_params=pltpu.CompilerParams(
            collective_id=0, has_side_effects=True, vmem_limit_bytes=56 * 1024 * 1024),
    )(projections, qk_gain, clusters.reshape(HEADS, 1, tokens), clusters, d_out, w_out)


def solution(mesh):
    ny = 4 if mesh.shape["seq"] == 64 else 2
    in_specs = (P("seq", "mp"), P(), P("mp", "seq", None), P("seq", None), P(None, "mp"))
    out_specs = (P("seq", "mp"), P("seq", "mp"))
    return jax.shard_map(functools.partial(per_device, ny), mesh=mesh, in_specs=in_specs,
                         out_specs=out_specs, check_vma=False)
```

```python
import functools

import jax
import jax.numpy as jnp
from jax import lax
from jax.experimental import pallas as pl
from jax.experimental.pallas import tpu as pltpu
from jax.sharding import PartitionSpec as P

EPSILON = 1e-06
HS = 128
HEADS = 2
CAP = 10
MAIN = 8
DEAD = 1024.0
TILE = 16
F32 = jnp.float32
BF16 = jnp.bfloat16

MAIN_ROW = (0, 32, 48, 64)
REST_ROW = 16
ROWS = 80
FIRST = 32


def dot(a, b, dims):
    return lax.dot_general(a, b, (dims, ((), ())), preferred_element_type=F32)


def normalize(raw):
    data = raw.astype(F32)
    inverse = lax.rsqrt(jnp.mean(data * data, axis=-1, keepdims=True) + EPSILON)
    return data * inverse, inverse


def norm_back(unit, inverse, gain, upstream):
    scaled = upstream * gain
    return inverse * (scaled - unit * jnp.mean(scaled * unit, axis=-1, keepdims=True))


def write_out(d_proj, d_w, d_proj_out, d_w_out):
    d_proj_out[...] = d_proj[...]
    d_w_out[...] = d_w[...]


def kernel(ny, nz, gain, ids_row, proj_in, d_out_in, w_out_in, d_proj, d_w,
           proj, d_out, w_out, sent, arrived, back1, back2, home1, home2, rest, d_cols, d_cols_t,
           att, att_all, part, out_r, out_l, in_r, in_l, qs, ks, vs, gs, low, grad_low,
           codes, chooser_t, in_sems, sems, ring_sems):
    n = ny * nz
    tokens = proj.shape[0]
    slots = n * CAP
    width = d_out.shape[1] // ny
    rows_z = width // nz
    me = lax.axis_index("seq")
    my_y, my_z = lax.div(me, nz), lax.rem(me, nz)

    def other(step):
        step = n - step
        j, dy = lax.div(step, ny), lax.rem(step, ny)
        dz = jnp.where(lax.rem(j, 2) == 1, lax.div(j + 1, 2), nz - lax.div(j, 2))
        return lax.rem(my_y + dy, ny) * nz + lax.rem(my_z + dz, nz)

    def along_y(dy):
        return lax.rem(my_y + dy, ny) * nz + my_z

    def copy_to(src, dst, send_sem, recv_sem, target):
        return pltpu.make_async_remote_copy(
            src_ref=src, dst_ref=dst, send_sem=send_sem, recv_sem=recv_sem,
            device_id={"seq": target}, device_id_type=pl.DeviceIdType.MESH)

    def remote(src, dst, number, target):
        return copy_to(src, dst, sems.at[2 * number], sems.at[2 * number + 1], target)

    def wait_for(ref, sem):
        pltpu.make_async_copy(ref, ref, sem).wait()

    def wait_sent(ref, number):
        wait_for(ref, sems.at[2 * number])

    def wait_arrived(ref, number):
        wait_for(ref, sems.at[2 * number + 1])

    loads = [pltpu.make_async_copy(src, dst, in_sems.at[i]) for i, (src, dst) in enumerate(
        ((proj_in, proj), (w_out_in, w_out), (d_out_in, d_out)))]
    for load in loads:
        load.start()
    barrier = pltpu.get_barrier_semaphore()

    @pl.loop(1, n)
    def _(step):
        pl.semaphore_signal(barrier, inc=1, device_id={"seq": other(step)},
                            device_id_type=pl.DeviceIdType.MESH)

    for load in loads:
        load.wait()

    grad_att = dot(d_out[...], w_out[...], ((1,), (0,))).astype(BF16)
    ones = jnp.ones((tokens, HS), BF16)
    packed = []
    for h in range(HEADS):
        first = h * 3 * HS
        q_unit, _ = normalize(proj[:, first:first + HS])
        k_unit, _ = normalize(proj[:, first + HS:first + 2 * HS])
        payload = jnp.concatenate(
            [(q_unit * gain[0:1, :]).astype(BF16), (k_unit * gain[1:2, :]).astype(BF16),
             proj[:, first + 2 * HS:first + 3 * HS], grad_att[:, h * HS:(h + 1) * HS], ones], axis=1)
        row = ids_row[h].astype(F32)
        col = jnp.broadcast_to(row, (tokens, tokens)).T
        t0 = lax.broadcasted_iota(jnp.int32, (tokens, tokens), 0)
        t1 = lax.broadcasted_iota(jnp.int32, (tokens, tokens), 1)
        rank = jnp.sum(jnp.where((row == col) & (t0 < t1), 1.0, 0.0), axis=0, keepdims=True)
        code = jnp.where(rank < MAIN, row * MAIN + rank, n * MAIN + (rank - MAIN) * n + row)
        codes[h] = code
        chooser = jnp.where(
            code.astype(jnp.int32) == lax.broadcasted_iota(jnp.int32, (slots, tokens), 0), 1.0, 0.0).astype(BF16)
        rows = dot(chooser, payload, ((1,), (0,)))
        live = rows[:, 4 * HS:]
        packed.append([rows[:, :HS], rows[:, HS:2 * HS],
                       rows[:, 2 * HS:3 * HS] + (1.0 - live) * DEAD, rows[:, 3 * HS:4 * HS]])

    def main_tile(parts, c):
        both = [parts[h][c][:n * MAIN].reshape(n, MAIN, HS) for h in range(HEADS)]
        return jnp.concatenate(both, axis=1).astype(BF16)

    def rest_tile(parts):
        for h in range(HEADS):
            for c in range(4):
                for r in range(CAP - MAIN):
                    start = n * (MAIN + r)
                    rest[pl.ds(c * 4 + h * 2 + r, n, stride=TILE), :] = parts[h][c][start:start + n]
        return rest[...].reshape(n, TILE, HS).astype(BF16)

    def slots_of(main, c, h):
        pieces = [main.astype(F32)[:, h * MAIN:(h + 1) * MAIN].reshape(n * MAIN, HS)]
        for r in range(CAP - MAIN):
            pieces.append(rest[pl.ds(c * 4 + h * 2 + r, n, stride=TILE), :])
        return jnp.concatenate(pieces, axis=0)

    for c in range(4):
        sent[:, MAIN_ROW[c]:MAIN_ROW[c] + TILE] = main_tile(packed, c)
    sent[:, REST_ROW:REST_ROW + TILE] = rest_tile(packed)

    pl.semaphore_wait(barrier, n - 1)

    @pl.loop(1, n)
    def _(step):
        target = other(step)
        remote(sent.at[target], arrived.at[me], 0, target).start()

    for dy in range(1, ny):
        start = pl.multiple_of(lax.rem(my_y + dy, ny) * width, width)
        remote(d_out.at[:, pl.ds(start, width)], d_cols.at[my_y], 1, along_y(dy)).start()
    own = pl.multiple_of(my_y * width, width)
    d_cols[my_y] = d_out[:, pl.ds(own, width)]
    arrived[me] = sent[me]
    for h in range(HEADS):
        code = jnp.broadcast_to(codes[h], (tokens, tokens)).T[:, 0:1].astype(jnp.int32)
        chooser_t[h] = jnp.where(
            code == lax.broadcasted_iota(jnp.int32, (tokens, slots), 1), 1.0, 0.0).astype(BF16)
    wait_arrived(d_cols.at[pl.ds(0, ny - 1)], 1)
    for y in range(ny):
        d_cols_t[:, y * tokens:(y + 1) * tokens] = d_cols[y].T

    wait_arrived(arrived.at[pl.ds(0, n - 1)], 0)

    rest[...] = arrived[:, REST_ROW:REST_ROW + TILE].astype(F32).reshape(n * TILE, HS)
    scale = HS ** -0.5
    results = []
    for h in range(HEADS):
        for c, ref in enumerate((qs, ks, vs, gs)):
            rows = slots_of(arrived[:, MAIN_ROW[c]:MAIN_ROW[c] + TILE], c, h)
            if c == 2:
                live = jnp.where(rows < DEAD / 2, 1.0, 0.0)[:, 0:1]
                rows = jnp.where(rows < DEAD / 2, rows, 0.0)
            ref[...] = rows.astype(BF16)
        out_t, grad_q_t = [], []
        for start in range(0, slots, 2 * HS):
            size = min(2 * HS, slots - start)
            block = slice(start, start + size)
            scores = dot(ks[...], qs[block], ((1,), (1,))) * scale
            expo = jnp.exp(scores) * live
            total = jnp.sum(expo, axis=0, keepdims=True)
            total = jnp.where(total == 0.0, 1.0, total)
            probs = expo / total
            probs_low = probs.astype(BF16)
            grad_probs = dot(vs[...], gs[block], ((1,), (1,)))
            row_dot = jnp.sum(probs * grad_probs, axis=0, keepdims=True)
            grad_scores = (probs * (grad_probs - row_dot) * scale).astype(BF16)
            low[:, block] = probs_low
            grad_low[:, block] = grad_scores
            out_t.append(dot(vs[...], probs_low, ((0,), (0,))))
            grad_q_t.append(dot(ks[...], grad_scores, ((0,), (0,))))
        out = jnp.concatenate(out_t, axis=1).T
        grad_q = jnp.concatenate(grad_q_t, axis=1).T
        grad_k = dot(grad_low[...], qs[...], ((1,), (0,)))
        grad_v = dot(low[...], gs[...], ((1,), (0,)))
        results.append([out, grad_q, grad_k, grad_v])
    back1[:, REST_ROW:REST_ROW + TILE] = rest_tile(results)
    back1[:, 0:TILE] = main_tile(results, 0)
    for c in range(1, 4):
        start = MAIN_ROW[c] - FIRST
        back2[:, start:start + TILE] = main_tile(results, c)

    @pl.loop(1, n)
    def _(step):
        target = other(step)
        remote(back1.at[target], home1.at[me], 2, target).start()

    bounds = [1 + (n - 1) * i // 10 for i in range(11)]

    def send_batch(i):
        @pl.loop(bounds[i], bounds[i + 1])
        def _(step):
            target = other(step)
            remote(back2.at[target], home2.at[me], 3, target).start()

    send_batch(0)
    home1[me] = back1[me]
    home2[me] = back2[me]

    wait_arrived(home1.at[pl.ds(0, n - 1)], 2)
    rest[...] = home1[:, REST_ROW:REST_ROW + TILE].astype(F32).reshape(n * TILE, HS)
    for h in range(HEADS):
        rows = slots_of(home1[:, 0:TILE], 0, h).astype(BF16)
        att[:, h * HS:(h + 1) * HS] = dot(chooser_t[h], rows, ((1,), (0,))).astype(BF16)
    for dy in range(1, ny):
        remote(att, att_all.at[my_y], 4, along_y(dy)).start()
    send_batch(1)
    att_all[my_y] = att[...]
    wait_arrived(att_all.at[pl.ds(0, ny - 1)], 4)
    gathered = att_all[...].reshape(ny * tokens, HEADS * HS)
    part[...] = dot(d_cols_t[...], gathered, ((1,), (0,)))

    half = nz // 2
    right = my_y * nz + lax.rem(my_z + 1, nz)
    left = my_y * nz + lax.rem(my_z + nz - 1, nz)

    def part_of(away):
        start = pl.multiple_of(lax.rem(my_z + away, nz) * rows_z, rows_z)
        return part[pl.ds(start, rows_z), :]

    def ring_copies(k):
        copies = [copy_to(out_r.at[k], in_r.at[k], ring_sems.at[0], ring_sems.at[2 + k], right)]
        if k < half - 1:
            copies.append(copy_to(out_l.at[k], in_l.at[k], ring_sems.at[1], ring_sems.at[2 + half + k], left))
        return copies

    for k in range(half):
        to_right, to_left = part_of(half - k), part_of(nz - half + 1 + k)
        if k > 0:
            to_right = to_right + in_r[k - 1].astype(F32)
            if k < half - 1:
                to_left = to_left + in_l[k - 1].astype(F32)
        out_r[k] = to_right.astype(BF16)
        if k < half - 1:
            out_l[k] = to_left.astype(BF16)
        for copy in ring_copies(k):
            copy.start()
        for i in range(2 + k * 8 // half, 2 + (k + 1) * 8 // half):
            send_batch(i)
        for copy in ring_copies(k):
            copy.wait_recv()
    total = part_of(0) + in_r[half - 1].astype(F32) + in_l[half - 2].astype(F32)
    d_w[...] = total * (tokens * n) ** -0.5

    wait_arrived(home2.at[pl.ds(0, n - 1)], 3)
    for h in range(HEADS):
        grads = []
        for c in range(1, 4):
            start = MAIN_ROW[c] - FIRST
            grads.append(slots_of(home2[:, start:start + TILE], c, h).astype(BF16))
        found = dot(chooser_t[h], jnp.concatenate(grads, axis=1), ((1,), (0,)))
        first = h * 3 * HS
        for c in range(2):
            unit, inverse = normalize(proj[:, first + c * HS:first + (c + 1) * HS])
            d_proj[:, first + c * HS:first + (c + 1) * HS] = norm_back(
                unit, inverse, gain[c:c + 1, :], found[:, c * HS:(c + 1) * HS]).astype(BF16)
        d_proj[:, first + 2 * HS:first + 3 * HS] = found[:, 2 * HS:].astype(BF16)

    wait_sent(sent.at[pl.ds(0, n - 1)], 0)
    wait_sent(d_cols.at[pl.ds(0, ny - 1)], 1)
    wait_sent(back1.at[pl.ds(0, n - 1)], 2)
    wait_sent(back2.at[pl.ds(0, n - 1)], 3)
    wait_sent(att_all.at[pl.ds(0, ny - 1)], 4)
    wait_for(out_r, ring_sems.at[0])
    wait_for(out_l, ring_sems.at[1])


def per_device(ny, projections, qk_gain, clusters, d_out, w_out):
    tokens = projections.shape[0]
    n = lax.axis_size("seq")
    nz = n // ny
    slots = n * CAP
    width = d_out.shape[1] // ny
    columns = HEADS * HS
    vmem = pltpu.VMEM
    half = nz // 2
    ring = (width // nz, columns)
    scratch = [
        vmem(projections.shape, BF16), vmem(d_out.shape, BF16), vmem(w_out.shape, BF16),
        vmem((n, ROWS, HS), BF16), vmem((n, ROWS, HS), BF16),
        vmem((n, FIRST, HS), BF16), vmem((n, ROWS - FIRST, HS), BF16),
        vmem((n, FIRST, HS), BF16), vmem((n, ROWS - FIRST, HS), BF16),
        vmem((n * TILE, HS), F32),
        vmem((ny, tokens, width), BF16), vmem((width, ny * tokens), BF16),
        vmem((tokens, columns), BF16), vmem((ny, tokens, columns), BF16),
        vmem((width, columns), F32),
        vmem((half, *ring), BF16), vmem((half - 1, *ring), BF16),
        vmem((half, *ring), BF16), vmem((half - 1, *ring), BF16),
        vmem((slots, HS), BF16), vmem((slots, HS), BF16), vmem((slots, HS), BF16), vmem((slots, HS), BF16),
        vmem((slots, slots), BF16), vmem((slots, slots), BF16),
        vmem((HEADS, 1, tokens), F32), vmem((HEADS, tokens, slots), BF16),
        pltpu.SemaphoreType.DMA((3,)), pltpu.SemaphoreType.DMA((10,)), pltpu.SemaphoreType.DMA((2 + nz - 1,)),
    ]
    whole = pl.BlockSpec(memory_space=pltpu.VMEM)
    anywhere = pl.BlockSpec(memory_space=pl.ANY)
    shapes = (jax.ShapeDtypeStruct(projections.shape, BF16),
              jax.ShapeDtypeStruct((width // nz, columns), F32))
    results = pl.pallas_call(
        functools.partial(kernel, ny, nz),
        out_shape=shapes,
        in_specs=[whole] * 2 + [anywhere] * 3,
        out_specs=(whole, whole),
        scratch_shapes=scratch,
        compiler_params=pltpu.CompilerParams(
            collective_id=0, has_side_effects=True, vmem_limit_bytes=56 * 1024 * 1024),
    )(qk_gain, clusters.reshape(HEADS, 1, tokens), projections, d_out, w_out)
    return pl.pallas_call(
        write_out, out_shape=shapes, in_specs=[whole] * 2, out_specs=(whole, whole))(*results)


def solution(mesh):
    ny = 4 if mesh.shape["seq"] == 64 else 2
    in_specs = (P("seq", "mp"), P(), P("mp", "seq", None), P("seq", None), P(None, "mp"))
    out_specs = (P("seq", "mp"), P("seq", "mp"))
    return jax.shard_map(functools.partial(per_device, ny), mesh=mesh, in_specs=in_specs,
                         out_specs=out_specs, check_vma=False)
```

```python
import functools

import jax
import jax.numpy as jnp
from jax import lax
from jax.experimental import pallas as pl
from jax.experimental.pallas import tpu as pltpu
from jax.sharding import PartitionSpec as P

EPSILON = 1e-06
HS = 128
HEADS = 2
CAP = 10
MAIN = 8
DEAD = 1024.0
TILE = 16
F32 = jnp.float32
BF16 = jnp.bfloat16

MAIN_ROW = (0, 32, 48, 64)
REST_ROW = 16
ROWS = 80
HALF = TILE // 2
FIRST = TILE + HALF
WEIGHTS = (0.12, 0.35)


def dot(a, b, dims):
    return lax.dot_general(a, b, (dims, ((), ())), preferred_element_type=F32)


def normalize(raw):
    data = raw.astype(F32)
    inverse = lax.rsqrt(jnp.mean(data * data, axis=-1, keepdims=True) + EPSILON)
    return data * inverse, inverse


def norm_back(unit, inverse, gain, upstream):
    scaled = upstream * gain
    return inverse * (scaled - unit * jnp.mean(scaled * unit, axis=-1, keepdims=True))


def write_out(d_proj, d_w, d_proj_out, d_w_out):
    d_proj_out[...] = d_proj[...]
    d_w_out[...] = d_w[...]


def batch_bounds(ny, nz, parts):
    n = ny * nz
    hops = [((n - step) // ny + 1) // 2 for step in range(1, n)]
    whole, bounds, done, share = sum(hops), [1], 0, 0.0
    for part in parts[:-1]:
        share += part
        step = bounds[-1]
        while step < n and done + hops[step - 1] / 2 <= share * whole:
            done += hops[step - 1]
            step += 1
        bounds.append(step)
    return bounds + [n]


def kernel(ny, nz, gain, ids_row, proj_in, d_out_in, w_out_in, d_proj, d_w,
           proj, d_out, w_out, sent, arrived, back1, back2, home1, home2, rest, rest1, rest2, d_cols, d_cols_t,
           att, att_all, part, out_r, out_l, in_r, in_l, qs, ks, vs, gs, low, grad_low,
           codes, chooser_t, in_sems, sems, ring_sems):
    n = ny * nz
    tokens = proj.shape[0]
    slots = n * CAP
    width = d_out.shape[1] // ny
    rows_z = width // nz
    me = lax.axis_index("seq")
    my_y, my_z = lax.div(me, nz), lax.rem(me, nz)

    def other(step, mirror=False):
        step = n - step
        j, dy = lax.div(step, ny), lax.rem(step, ny)
        dz = jnp.where(lax.rem(j, 2) == 1, lax.div(j + 1, 2), nz - lax.div(j, 2))
        if mirror:
            dz = jnp.where(2 * dy < ny, dz, 2 * nz - dz)
        return lax.rem(my_y + dy, ny) * nz + lax.rem(my_z + dz, nz)

    def along_y(dy):
        return lax.rem(my_y + dy, ny) * nz + my_z

    def copy_to(src, dst, send_sem, recv_sem, target):
        return pltpu.make_async_remote_copy(
            src_ref=src, dst_ref=dst, send_sem=send_sem, recv_sem=recv_sem,
            device_id={"seq": target}, device_id_type=pl.DeviceIdType.MESH)

    def remote(src, dst, number, target):
        return copy_to(src, dst, sems.at[2 * number], sems.at[2 * number + 1], target)

    def wait_for(ref, sem):
        pltpu.make_async_copy(ref, ref, sem).wait()

    def wait_sent(ref, number):
        wait_for(ref, sems.at[2 * number])

    def wait_arrived(ref, number):
        wait_for(ref, sems.at[2 * number + 1])

    loads = [pltpu.make_async_copy(src, dst, in_sems.at[i]) for i, (src, dst) in enumerate(
        ((proj_in, proj), (w_out_in, w_out), (d_out_in, d_out)))]
    for load in loads:
        load.start()
    barrier = pltpu.get_barrier_semaphore()

    @pl.loop(1, n)
    def _(step):
        pl.semaphore_signal(barrier, inc=1, device_id={"seq": other(step)},
                            device_id_type=pl.DeviceIdType.MESH)

    for load in loads:
        load.wait()

    grad_att = dot(d_out[...], w_out[...], ((1,), (0,))).astype(BF16)
    ones = jnp.ones((tokens, HS), BF16)
    packed = []
    for h in range(HEADS):
        first = h * 3 * HS
        q_unit, _ = normalize(proj[:, first:first + HS])
        k_unit, _ = normalize(proj[:, first + HS:first + 2 * HS])
        payload = jnp.concatenate(
            [(q_unit * gain[0:1, :]).astype(BF16), (k_unit * gain[1:2, :]).astype(BF16),
             proj[:, first + 2 * HS:first + 3 * HS], grad_att[:, h * HS:(h + 1) * HS], ones], axis=1)
        row = ids_row[h].astype(F32)
        col = jnp.broadcast_to(row, (tokens, tokens)).T
        t0 = lax.broadcasted_iota(jnp.int32, (tokens, tokens), 0)
        t1 = lax.broadcasted_iota(jnp.int32, (tokens, tokens), 1)
        rank = jnp.sum(jnp.where((row == col) & (t0 < t1), 1.0, 0.0), axis=0, keepdims=True)
        code = jnp.where(rank < MAIN, row * MAIN + rank, n * MAIN + (rank - MAIN) * n + row)
        codes[h] = code
        chooser = jnp.where(
            code.astype(jnp.int32) == lax.broadcasted_iota(jnp.int32, (slots, tokens), 0), 1.0, 0.0).astype(BF16)
        rows = dot(chooser, payload, ((1,), (0,)))
        live = rows[:, 4 * HS:]
        packed.append([rows[:, :HS], rows[:, HS:2 * HS],
                       rows[:, 2 * HS:3 * HS] + (1.0 - live) * DEAD, rows[:, 3 * HS:4 * HS]])

    def main_tile(parts, c):
        both = [parts[h][c][:n * MAIN].reshape(n, MAIN, HS) for h in range(HEADS)]
        return jnp.concatenate(both, axis=1).astype(BF16)

    def fill_rest(parts):
        for h in range(HEADS):
            for c in range(4):
                for r in range(CAP - MAIN):
                    start = n * (MAIN + r)
                    rest[pl.ds(c * 4 + h * 2 + r, n, stride=TILE), :] = parts[h][c][start:start + n]
        return rest[...].reshape(n, TILE, HS).astype(BF16)

    def slots_of(main, c, h, rest=rest, stride=TILE):
        pieces = [main.astype(F32)[:, h * MAIN:(h + 1) * MAIN].reshape(n * MAIN, HS)]
        for r in range(CAP - MAIN):
            pieces.append(rest[pl.ds(c * 4 + h * 2 + r, n, stride=stride), :])
        return jnp.concatenate(pieces, axis=0)

    for c in range(4):
        sent[:, MAIN_ROW[c]:MAIN_ROW[c] + TILE] = main_tile(packed, c)
    sent[:, REST_ROW:REST_ROW + TILE] = fill_rest(packed)

    pl.semaphore_wait(barrier, n - 1)

    @pl.loop(1, n)
    def _(step):
        target = other(step)
        remote(sent.at[target], arrived.at[me], 0, target).start()

    for dy in range(1, ny):
        start = pl.multiple_of(lax.rem(my_y + dy, ny) * width, width)
        remote(d_out.at[:, pl.ds(start, width)], d_cols.at[my_y], 1, along_y(dy)).start()
    own = pl.multiple_of(my_y * width, width)
    d_cols[my_y] = d_out[:, pl.ds(own, width)]
    arrived[me] = sent[me]
    for h in range(HEADS):
        code = jnp.broadcast_to(codes[h], (tokens, tokens)).T[:, 0:1].astype(jnp.int32)
        chooser_t[h] = jnp.where(
            code == lax.broadcasted_iota(jnp.int32, (tokens, slots), 1), 1.0, 0.0).astype(BF16)
    wait_arrived(d_cols.at[pl.ds(0, ny - 1)], 1)
    for y in range(ny):
        d_cols_t[:, y * tokens:(y + 1) * tokens] = d_cols[y].T

    wait_arrived(arrived.at[pl.ds(0, n - 1)], 0)

    rest[...] = arrived[:, REST_ROW:REST_ROW + TILE].astype(F32).reshape(n * TILE, HS)
    scale = HS ** -0.5
    results = []
    for h in range(HEADS):
        for c, ref in enumerate((qs, ks, vs, gs)):
            rows = slots_of(arrived[:, MAIN_ROW[c]:MAIN_ROW[c] + TILE], c, h)
            if c == 2:
                live = jnp.where(rows < DEAD / 2, 1.0, 0.0)[:, 0:1]
                rows = jnp.where(rows < DEAD / 2, rows, 0.0)
            ref[...] = rows.astype(BF16)
        out_t, grad_q_t = [], []
        for start in range(0, slots, 2 * HS):
            size = min(2 * HS, slots - start)
            block = slice(start, start + size)
            scores = dot(ks[...], qs[block], ((1,), (1,))) * scale
            expo = jnp.exp(scores) * live
            total = jnp.sum(expo, axis=0, keepdims=True)
            total = jnp.where(total == 0.0, 1.0, total)
            probs = expo / total
            probs_low = probs.astype(BF16)
            grad_probs = dot(vs[...], gs[block], ((1,), (1,)))
            row_dot = jnp.sum(probs * grad_probs, axis=0, keepdims=True)
            grad_scores = (probs * (grad_probs - row_dot) * scale).astype(BF16)
            low[:, block] = probs_low
            grad_low[:, block] = grad_scores
            out_t.append(dot(vs[...], probs_low, ((0,), (0,))))
            grad_q_t.append(dot(ks[...], grad_scores, ((0,), (0,))))
        out = jnp.concatenate(out_t, axis=1).T
        grad_q = jnp.concatenate(grad_q_t, axis=1).T
        grad_k = dot(grad_low[...], qs[...], ((1,), (0,)))
        grad_v = dot(low[...], gs[...], ((1,), (0,)))
        results.append([out, grad_q, grad_k, grad_v])
    back_rest = fill_rest(results)
    back1[:, 0:TILE] = main_tile(results, 0)
    back1[:, TILE:] = back_rest[:, :HALF]
    for c in range(1, 4):
        back2[:, (c - 1) * TILE:c * TILE] = main_tile(results, c)
    back2[:, 3 * TILE:] = back_rest[:, HALF:]

    @pl.loop(1, n)
    def _(step):
        target = other(step)
        remote(back1.at[target], home1.at[me], 2, target).start()

    bounds = batch_bounds(ny, nz, WEIGHTS + ((1 - sum(WEIGHTS)) / (nz // 2),) * (nz // 2))

    def send_batch(i):
        @pl.loop(bounds[i], bounds[i + 1])
        def _(step):
            target = other(step, mirror=True)
            remote(back2.at[target], home2.at[me], 3, target).start()

    send_batch(0)
    home1[me] = back1[me]
    home2[me] = back2[me]

    wait_arrived(home1.at[pl.ds(0, n - 1)], 2)
    rest1[...] = home1[:, TILE:].astype(F32).reshape(n * HALF, HS)
    for h in range(HEADS):
        rows = slots_of(home1[:, 0:TILE], 0, h, rest1, HALF).astype(BF16)
        att[:, h * HS:(h + 1) * HS] = dot(chooser_t[h], rows, ((1,), (0,))).astype(BF16)
    for dy in range(1, ny):
        remote(att, att_all.at[my_y], 4, along_y(dy)).start()
    send_batch(1)
    att_all[my_y] = att[...]
    wait_arrived(att_all.at[pl.ds(0, ny - 1)], 4)
    gathered = att_all[...].reshape(ny * tokens, HEADS * HS)
    part[...] = dot(d_cols_t[...], gathered, ((1,), (0,)))

    half = nz // 2
    right = my_y * nz + lax.rem(my_z + 1, nz)
    left = my_y * nz + lax.rem(my_z + nz - 1, nz)

    def part_of(away):
        start = pl.multiple_of(lax.rem(my_z + away, nz) * rows_z, rows_z)
        return part[pl.ds(start, rows_z), :]

    def ring_copies(k):
        copies = [copy_to(out_r.at[k], in_r.at[k], ring_sems.at[0], ring_sems.at[2 + k], right)]
        if k < half - 1:
            copies.append(copy_to(out_l.at[k], in_l.at[k], ring_sems.at[1], ring_sems.at[2 + half + k], left))
        return copies

    for k in range(half):
        to_right, to_left = part_of(half - k), part_of(nz - half + 1 + k)
        if k > 0:
            to_right = to_right + in_r[k - 1].astype(F32)
            if k < half - 1:
                to_left = to_left + in_l[k - 1].astype(F32)
        out_r[k] = to_right.astype(BF16)
        if k < half - 1:
            out_l[k] = to_left.astype(BF16)
        for copy in ring_copies(k):
            copy.start()
        send_batch(len(WEIGHTS) + k)
        for copy in ring_copies(k):
            copy.wait_recv()
    total = part_of(0) + in_r[half - 1].astype(F32) + in_l[half - 2].astype(F32)
    d_w[...] = total * (tokens * n) ** -0.5

    wait_arrived(home2.at[pl.ds(0, n - 1)], 3)
    rest2[...] = home2[:, 3 * TILE:].astype(F32).reshape(n * HALF, HS)
    for h in range(HEADS):
        grads = []
        for c in range(1, 4):
            main = home2[:, (c - 1) * TILE:c * TILE]
            spare = rest1 if c == 1 else rest2
            grads.append(slots_of(main, c if c == 1 else c - 2, h, spare, HALF).astype(BF16))
        found = dot(chooser_t[h], jnp.concatenate(grads, axis=1), ((1,), (0,)))
        first = h * 3 * HS
        for c in range(2):
            unit, inverse = normalize(proj[:, first + c * HS:first + (c + 1) * HS])
            d_proj[:, first + c * HS:first + (c + 1) * HS] = norm_back(
                unit, inverse, gain[c:c + 1, :], found[:, c * HS:(c + 1) * HS]).astype(BF16)
        d_proj[:, first + 2 * HS:first + 3 * HS] = found[:, 2 * HS:].astype(BF16)

    wait_sent(sent.at[pl.ds(0, n - 1)], 0)
    wait_sent(d_cols.at[pl.ds(0, ny - 1)], 1)
    wait_sent(back1.at[pl.ds(0, n - 1)], 2)
    wait_sent(back2.at[pl.ds(0, n - 1)], 3)
    wait_sent(att_all.at[pl.ds(0, ny - 1)], 4)
    wait_for(out_r, ring_sems.at[0])
    wait_for(out_l, ring_sems.at[1])


def per_device(ny, projections, qk_gain, clusters, d_out, w_out):
    tokens = projections.shape[0]
    n = lax.axis_size("seq")
    nz = n // ny
    slots = n * CAP
    width = d_out.shape[1] // ny
    columns = HEADS * HS
    vmem = pltpu.VMEM
    half = nz // 2
    ring = (width // nz, columns)
    scratch = [
        vmem(projections.shape, BF16), vmem(d_out.shape, BF16), vmem(w_out.shape, BF16),
        vmem((n, ROWS, HS), BF16), vmem((n, ROWS, HS), BF16),
        vmem((n, FIRST, HS), BF16), vmem((n, ROWS - FIRST, HS), BF16),
        vmem((n, FIRST, HS), BF16), vmem((n, ROWS - FIRST, HS), BF16),
        vmem((n * TILE, HS), F32), vmem((n * HALF, HS), F32), vmem((n * HALF, HS), F32),
        vmem((ny, tokens, width), BF16), vmem((width, ny * tokens), BF16),
        vmem((tokens, columns), BF16), vmem((ny, tokens, columns), BF16),
        vmem((width, columns), F32),
        vmem((half, *ring), BF16), vmem((half - 1, *ring), BF16),
        vmem((half, *ring), BF16), vmem((half - 1, *ring), BF16),
        vmem((slots, HS), BF16), vmem((slots, HS), BF16), vmem((slots, HS), BF16), vmem((slots, HS), BF16),
        vmem((slots, slots), BF16), vmem((slots, slots), BF16),
        vmem((HEADS, 1, tokens), F32), vmem((HEADS, tokens, slots), BF16),
        pltpu.SemaphoreType.DMA((3,)), pltpu.SemaphoreType.DMA((10,)), pltpu.SemaphoreType.DMA((2 + nz - 1,)),
    ]
    whole = pl.BlockSpec(memory_space=pltpu.VMEM)
    anywhere = pl.BlockSpec(memory_space=pl.ANY)
    shapes = (jax.ShapeDtypeStruct(projections.shape, BF16),
              jax.ShapeDtypeStruct((width // nz, columns), F32))
    results = pl.pallas_call(
        functools.partial(kernel, ny, nz),
        out_shape=shapes,
        in_specs=[whole] * 2 + [anywhere] * 3,
        out_specs=(whole, whole),
        scratch_shapes=scratch,
        compiler_params=pltpu.CompilerParams(
            collective_id=0, has_side_effects=True, vmem_limit_bytes=56 * 1024 * 1024),
    )(qk_gain, clusters.reshape(HEADS, 1, tokens), projections, d_out, w_out)
    return pl.pallas_call(
        write_out, out_shape=shapes, in_specs=[whole] * 2, out_specs=(whole, whole))(*results)


def solution(mesh):
    ny = 4 if mesh.shape["seq"] == 64 else 2
    in_specs = (P("seq", "mp"), P(), P("mp", "seq", None), P("seq", None), P(None, "mp"))
    out_specs = (P("seq", "mp"), P("seq", "mp"))
    return jax.shard_map(functools.partial(per_device, ny), mesh=mesh, in_specs=in_specs,
                         out_specs=out_specs, check_vma=False)
```

```python
import functools

import jax
import jax.numpy as jnp
from jax import lax
from jax.experimental import pallas as pl
from jax.experimental.pallas import tpu as pltpu
from jax.sharding import PartitionSpec as P

EPSILON = 1e-06
HS = 128
HEADS = 2
CAP = 10
MAIN = 8
DEAD = 1024.0
F32 = jnp.float32
BF16 = jnp.bfloat16

BLOCK = 8
OUT_BLOCKS = 5
BACK = (((0, 2),), ((0, 0), (1, 0)), ((0, 1), (1, 1), (1, 2), (0, 3), (1, 3)))
REST = (False, True, True)
WEIGHTS = (0.15, 0.35, 0.15)


def dot(a, b, dims):
    return lax.dot_general(a, b, (dims, ((), ())), preferred_element_type=F32)


def normalize(raw):
    data = raw.astype(F32)
    inverse = lax.rsqrt(jnp.mean(data * data, axis=-1, keepdims=True) + EPSILON)
    return data * inverse, inverse


def norm_back(unit, inverse, gain, upstream):
    scaled = upstream * gain
    return inverse * (scaled - unit * jnp.mean(scaled * unit, axis=-1, keepdims=True))


def write_out(d_proj, d_w, d_proj_out, d_w_out):
    d_proj_out[...] = d_proj[...]
    d_w_out[...] = d_w[...]


def batch_bounds(ny, nz, parts):
    n = ny * nz
    hops = [((n - step) // ny + 1) // 2 for step in range(1, n)]
    whole, bounds, done, share = sum(hops), [1], 0, 0.0
    for part in parts[:-1]:
        share += part
        step = bounds[-1]
        while step < n and done + hops[step - 1] / 2 <= share * whole:
            done += hops[step - 1]
            step += 1
        bounds.append(step)
    return bounds + [n]


def kernel(ny, nz, gain, ids_row, proj_in, d_out_in, w_out_in, d_proj, d_w,
           proj, d_out, w_out, sent, arrived, back0, back1, back2, home0, home1, home2,
           rest, rest_a, rest_b, d_cols, d_cols_t, att, att_all, part, mine, pair_out, pair_in,
           out_r, out_l, in_r, in_l, qs, ks, vs, gs, low, grad_low,
           codes, chooser_t, in_sems, sems, ring_sems):
    n = ny * nz
    tokens = proj.shape[0]
    slots = n * CAP
    width = d_out.shape[1] // ny
    rows_z = width // nz
    me = lax.axis_index("seq")
    my_y, my_z = lax.div(me, nz), lax.rem(me, nz)

    def other(step, mirror=False):
        step = n - step
        j, dy = lax.div(step, ny), lax.rem(step, ny)
        dz = jnp.where(lax.rem(j, 2) == 1, lax.div(j + 1, 2), nz - lax.div(j, 2))
        if mirror:
            dz = jnp.where(2 * dy < ny, dz, 2 * nz - dz)
        return lax.rem(my_y + dy, ny) * nz + lax.rem(my_z + dz, nz)

    def along_y(dy):
        return lax.rem(my_y + dy, ny) * nz + my_z

    def copy_to(src, dst, send_sem, recv_sem, target):
        return pltpu.make_async_remote_copy(
            src_ref=src, dst_ref=dst, send_sem=send_sem, recv_sem=recv_sem,
            device_id={"seq": target}, device_id_type=pl.DeviceIdType.MESH)

    def remote(src, dst, number, target):
        return copy_to(src, dst, sems.at[2 * number], sems.at[2 * number + 1], target)

    def wait_for(ref, sem):
        pltpu.make_async_copy(ref, ref, sem).wait()

    def wait_sent(ref, number):
        wait_for(ref, sems.at[2 * number])

    def wait_arrived(ref, number):
        wait_for(ref, sems.at[2 * number + 1])

    loads = [pltpu.make_async_copy(src, dst, in_sems.at[i]) for i, (src, dst) in enumerate(
        ((proj_in, proj), (w_out_in, w_out), (d_out_in, d_out)))]
    for load in loads:
        load.start()
    barrier = pltpu.get_barrier_semaphore()

    @pl.loop(1, n)
    def _(step):
        pl.semaphore_signal(barrier, inc=1, device_id={"seq": other(step)},
                            device_id_type=pl.DeviceIdType.MESH)

    for load in loads:
        load.wait()

    grad_att = dot(d_out[...], w_out[...], ((1,), (0,))).astype(BF16)
    ones = jnp.ones((tokens, HS), BF16)

    def main_block(rows):
        return rows[:n * MAIN].reshape(n, MAIN, HS)

    def put_rest(ref, at, rows):
        for r in range(CAP - MAIN):
            start = n * (MAIN + r)
            ref[pl.ds(at + r, n, stride=BLOCK), :] = rows[start:start + n]

    def rest_block(ref):
        return ref[...].reshape(n, BLOCK, HS)

    def slots_of(block, ref, at):
        pieces = [block.reshape(n * MAIN, HS)]
        for r in range(CAP - MAIN):
            pieces.append(ref[pl.ds(at + r, n, stride=BLOCK), :])
        return jnp.concatenate(pieces, axis=0)

    def block_of(message, i):
        return message[:, i * BLOCK:(i + 1) * BLOCK]

    def to_all(src, dst, number, steps=(1, n), mirror=False):
        @pl.loop(*steps)
        def _(step):
            target = other(step, mirror)
            remote(src.at[target], dst.at[me], number, target).start()

    def pack(h):
        first = h * 3 * HS
        q_unit, _ = normalize(proj[:, first:first + HS])
        k_unit, _ = normalize(proj[:, first + HS:first + 2 * HS])
        payload = jnp.concatenate(
            [(q_unit * gain[0:1, :]).astype(BF16), (k_unit * gain[1:2, :]).astype(BF16),
             proj[:, first + 2 * HS:first + 3 * HS], grad_att[:, h * HS:(h + 1) * HS], ones], axis=1)
        row = ids_row[h].astype(F32)
        col = jnp.broadcast_to(row, (tokens, tokens)).T
        t0 = lax.broadcasted_iota(jnp.int32, (tokens, tokens), 0)
        t1 = lax.broadcasted_iota(jnp.int32, (tokens, tokens), 1)
        rank = jnp.sum(jnp.where((row == col) & (t0 < t1), 1.0, 0.0), axis=0, keepdims=True)
        code = jnp.where(rank < MAIN, row * MAIN + rank, n * MAIN + (rank - MAIN) * n + row)
        codes[h] = code
        chooser = jnp.where(
            code.astype(jnp.int32) == lax.broadcasted_iota(jnp.int32, (slots, tokens), 0), 1.0, 0.0).astype(BF16)
        rows = dot(chooser, payload, ((1,), (0,)))
        live = rows[:, 4 * HS:]
        parts = [rows[:, :HS], rows[:, HS:2 * HS],
                 rows[:, 2 * HS:3 * HS] + (1.0 - live) * DEAD, rows[:, 3 * HS:4 * HS]]
        for c in range(4):
            put_rest(rest, c * 2, parts[c])
        sent[h] = jnp.concatenate([main_block(p) for p in parts] + [rest_block(rest)], axis=1).astype(BF16)

    pack(0)
    pl.semaphore_wait(barrier, n - 1)
    to_all(sent.at[0], arrived.at[0], 0)
    pack(1)
    to_all(sent.at[1], arrived.at[1], 1)

    for dy in range(1, ny):
        start = pl.multiple_of(lax.rem(my_y + dy, ny) * width, width)
        remote(d_out.at[:, pl.ds(start, width)], d_cols.at[my_y], 2, along_y(dy)).start()
    own = pl.multiple_of(my_y * width, width)
    d_cols[my_y] = d_out[:, pl.ds(own, width)]
    for h in range(HEADS):
        arrived[h, me] = sent[h, me]
        code = jnp.broadcast_to(codes[h], (tokens, tokens)).T[:, 0:1].astype(jnp.int32)
        chooser_t[h] = jnp.where(
            code == lax.broadcasted_iota(jnp.int32, (tokens, slots), 1), 1.0, 0.0).astype(BF16)

    scale = HS ** -0.5

    def own_cluster(h):
        message = arrived[h].astype(F32)
        rest[...] = block_of(message, OUT_BLOCKS - 1).reshape(n * BLOCK, HS)
        for c, ref in enumerate((qs, ks, vs, gs)):
            rows = slots_of(block_of(message, c), rest, c * 2)
            if c == 2:
                live = jnp.where(rows < DEAD / 2, 1.0, 0.0)[:, 0:1]
                rows = jnp.where(rows < DEAD / 2, rows, 0.0)
            ref[...] = rows.astype(BF16)
        out_t, grad_q_t = [], []
        for start in range(0, slots, 2 * HS):
            size = min(2 * HS, slots - start)
            block = slice(start, start + size)
            scores = dot(ks[...], qs[block], ((1,), (1,))) * scale
            expo = jnp.exp(scores) * live
            total = jnp.sum(expo, axis=0, keepdims=True)
            total = jnp.where(total == 0.0, 1.0, total)
            probs = expo / total
            probs_low = probs.astype(BF16)
            grad_probs = dot(vs[...], gs[block], ((1,), (1,)))
            row_dot = jnp.sum(probs * grad_probs, axis=0, keepdims=True)
            grad_scores = (probs * (grad_probs - row_dot) * scale).astype(BF16)
            low[:, block] = probs_low
            grad_low[:, block] = grad_scores
            out_t.append(dot(vs[...], probs_low, ((0,), (0,))))
            grad_q_t.append(dot(ks[...], grad_scores, ((0,), (0,))))
        out = jnp.concatenate(out_t, axis=1).T
        grad_q = jnp.concatenate(grad_q_t, axis=1).T
        grad_k = dot(grad_low[...], qs[...], ((1,), (0,)))
        grad_v = dot(low[...], gs[...], ((1,), (0,)))
        parts = [out, grad_q, grad_k, grad_v]
        for c in range(4):
            put_rest(rest_a if c < 2 else rest_b, c % 2 * 4 + h * 2, parts[c])
        return [main_block(p) for p in parts]

    def message_back(i, results):
        blocks = [results[h][c] for h, c in BACK[i]]
        if REST[i]:
            blocks.append(rest_block(rest_a if i == 1 else rest_b))
        return jnp.concatenate(blocks, axis=1).astype(BF16)

    wait_arrived(arrived.at[0, pl.ds(0, n - 1)], 0)
    results = [own_cluster(0)]
    back0[...] = message_back(0, results)
    to_all(back0, home0, 3)
    home0[me] = back0[me]
    wait_arrived(d_cols.at[pl.ds(0, ny - 1)], 2)
    for y in range(ny):
        d_cols_t[:, y * tokens:(y + 1) * tokens] = d_cols[y].T
    wait_arrived(arrived.at[1, pl.ds(0, n - 1)], 1)
    results.append(own_cluster(1))
    back1[...] = message_back(1, results)
    to_all(back1, home1, 4)
    back2[...] = message_back(2, results)

    members = nz // 2
    half = members // 2
    bounds = batch_bounds(ny, nz, WEIGHTS + ((1 - sum(WEIGHTS)) / half,) * half)

    def send_batch(i):
        to_all(back2, home2, 5, (bounds[i], bounds[i + 1]), mirror=True)

    send_batch(0)
    home1[me] = back1[me]
    home2[me] = back2[me]

    wait_arrived(home1.at[pl.ds(0, n - 1)], 4)
    message = home1[...].astype(F32)
    rest_a[...] = block_of(message, len(BACK[1])).reshape(n * BLOCK, HS)
    for h in range(HEADS):
        rows = slots_of(block_of(message, h), rest_a, h * 2).astype(BF16)
        att[:, h * HS:(h + 1) * HS] = dot(chooser_t[h], rows, ((1,), (0,))).astype(BF16)
    for dy in range(1, ny):
        remote(att, att_all.at[my_y], 6, along_y(dy)).start()
    send_batch(1)
    att_all[my_y] = att[...]
    wait_arrived(att_all.at[pl.ds(0, ny - 1)], 6)
    gathered = att_all[...].reshape(ny * tokens, HEADS * HS)
    part[...] = dot(d_cols_t[...], gathered, ((1,), (0,))).reshape(members, 2, rows_z, HEADS * HS)

    odd = lax.rem(my_z, 2)
    for h in range(HEADS):
        side = 1 - 2 * odd if h == 0 else 2 * odd - 1
        partner = my_y * nz + lax.rem(my_z + side + nz, nz)
        pair_out[h] = part[:, 1 - odd, :, h * HS:(h + 1) * HS].astype(BF16)
        remote(pair_out.at[h], pair_in.at[h], 7 + h, partner).start()
    send_batch(2)
    for h in range(HEADS):
        wait_arrived(pair_in.at[h], 7 + h)
        mine[:, :, h * HS:(h + 1) * HS] = part[:, odd, :, h * HS:(h + 1) * HS] + pair_in[h].astype(F32)

    my_place = lax.div(my_z, 2)
    right = my_y * nz + lax.rem(my_z + 2, nz)
    left = my_y * nz + lax.rem(my_z + nz - 2, nz)

    def part_of(away):
        return mine[lax.rem(my_place + away, members)]

    def ring_copies(k):
        copies = [copy_to(out_r.at[k], in_r.at[k], ring_sems.at[0], ring_sems.at[2 + k], right)]
        if k < half - 1:
            copies.append(copy_to(out_l.at[k], in_l.at[k], ring_sems.at[1], ring_sems.at[2 + half + k], left))
        return copies

    for k in range(half):
        to_right, to_left = part_of(half - k), part_of(members - half + 1 + k)
        if k > 0:
            to_right = to_right + in_r[k - 1].astype(F32)
            if k < half - 1:
                to_left = to_left + in_l[k - 1].astype(F32)
        out_r[k] = to_right.astype(BF16)
        if k < half - 1:
            out_l[k] = to_left.astype(BF16)
        for copy in ring_copies(k):
            copy.start()
        send_batch(len(WEIGHTS) + k)
        for copy in ring_copies(k):
            copy.wait_recv()
    total = part_of(0) + in_r[half - 1].astype(F32) + in_l[half - 2].astype(F32)
    d_w[...] = total * (tokens * n) ** -0.5

    wait_arrived(home0.at[pl.ds(0, n - 1)], 3)
    wait_arrived(home2.at[pl.ds(0, n - 1)], 5)
    first_message, message = home0[...].astype(F32), home2[...].astype(F32)
    rest_b[...] = block_of(message, len(BACK[2])).reshape(n * BLOCK, HS)
    for h in range(HEADS):
        grads = []
        for c in range(1, 4):
            block = first_message if (h, c) in BACK[0] else block_of(message, BACK[2].index((h, c)))
            grads.append(slots_of(block, rest_a if c < 2 else rest_b, c % 2 * 4 + h * 2).astype(BF16))
        found = dot(chooser_t[h], jnp.concatenate(grads, axis=1), ((1,), (0,)))
        first = h * 3 * HS
        for c in range(2):
            unit, inverse = normalize(proj[:, first + c * HS:first + (c + 1) * HS])
            d_proj[:, first + c * HS:first + (c + 1) * HS] = norm_back(
                unit, inverse, gain[c:c + 1, :], found[:, c * HS:(c + 1) * HS]).astype(BF16)
        d_proj[:, first + 2 * HS:first + 3 * HS] = found[:, 2 * HS:].astype(BF16)

    for h in range(HEADS):
        wait_sent(sent.at[h, pl.ds(0, n - 1)], h)
    wait_sent(d_cols.at[pl.ds(0, ny - 1)], 2)
    wait_sent(back0.at[pl.ds(0, n - 1)], 3)
    wait_sent(back1.at[pl.ds(0, n - 1)], 4)
    wait_sent(back2.at[pl.ds(0, n - 1)], 5)
    wait_sent(att_all.at[pl.ds(0, ny - 1)], 6)
    for h in range(HEADS):
        wait_sent(pair_out.at[h], 7 + h)
    wait_for(out_r, ring_sems.at[0])
    wait_for(out_l, ring_sems.at[1])


def per_device(ny, projections, qk_gain, clusters, d_out, w_out):
    tokens = projections.shape[0]
    n = lax.axis_size("seq")
    nz = n // ny
    slots = n * CAP
    width = d_out.shape[1] // ny
    columns = HEADS * HS
    vmem = pltpu.VMEM
    members = nz // 2
    half = members // 2
    rows_z = width // nz
    ring = (rows_z, columns)
    back = [vmem((n, (len(BACK[i]) + REST[i]) * BLOCK, HS), BF16) for i in range(3)]
    rest = vmem((n * BLOCK, HS), F32)
    scratch = [
        vmem(projections.shape, BF16), vmem(d_out.shape, BF16), vmem(w_out.shape, BF16),
        vmem((HEADS, n, OUT_BLOCKS * BLOCK, HS), BF16), vmem((HEADS, n, OUT_BLOCKS * BLOCK, HS), BF16),
        *back, *back, rest, rest, rest,
        vmem((ny, tokens, width), BF16), vmem((width, ny * tokens), BF16),
        vmem((tokens, columns), BF16), vmem((ny, tokens, columns), BF16),
        vmem((members, 2, *ring), F32), vmem((members, *ring), F32),
        vmem((HEADS, members, rows_z, HS), BF16), vmem((HEADS, members, rows_z, HS), BF16),
        vmem((half, *ring), BF16), vmem((half - 1, *ring), BF16),
        vmem((half, *ring), BF16), vmem((half - 1, *ring), BF16),
        vmem((slots, HS), BF16), vmem((slots, HS), BF16), vmem((slots, HS), BF16), vmem((slots, HS), BF16),
        vmem((slots, slots), BF16), vmem((slots, slots), BF16),
        vmem((HEADS, 1, tokens), F32), vmem((HEADS, tokens, slots), BF16),
        pltpu.SemaphoreType.DMA((3,)), pltpu.SemaphoreType.DMA((18,)), pltpu.SemaphoreType.DMA((2 + members - 1,)),
    ]
    whole = pl.BlockSpec(memory_space=pltpu.VMEM)
    anywhere = pl.BlockSpec(memory_space=pl.ANY)
    shapes = (jax.ShapeDtypeStruct(projections.shape, BF16),
              jax.ShapeDtypeStruct((width // nz, columns), F32))
    results = pl.pallas_call(
        functools.partial(kernel, ny, nz),
        out_shape=shapes,
        in_specs=[whole] * 2 + [anywhere] * 3,
        out_specs=(whole, whole),
        scratch_shapes=scratch,
        compiler_params=pltpu.CompilerParams(
            collective_id=0, has_side_effects=True, vmem_limit_bytes=56 * 1024 * 1024),
    )(qk_gain, clusters.reshape(HEADS, 1, tokens), projections, d_out, w_out)
    return pl.pallas_call(
        write_out, out_shape=shapes, in_specs=[whole] * 2, out_specs=(whole, whole))(*results)


def solution(mesh):
    ny = 4 if mesh.shape["seq"] == 64 else 2
    in_specs = (P("seq", "mp"), P(), P("mp", "seq", None), P("seq", None), P(None, "mp"))
    out_specs = (P("seq", "mp"), P("seq", "mp"))
    return jax.shard_map(functools.partial(per_device, ny), mesh=mesh, in_specs=in_specs,
                         out_specs=out_specs, check_vma=False)
```

```python
import functools

import jax
import jax.numpy as jnp
from jax import lax
from jax.experimental import pallas as pl
from jax.experimental.pallas import tpu as pltpu
from jax.sharding import PartitionSpec as P

EPSILON = 1e-06
HS = 128
HEADS = 2
CAP = 10
MAIN = 8
DEAD = 1024.0
F32 = jnp.float32
BF16 = jnp.bfloat16

BLOCK = 8
OUT_BLOCKS = 5
BACK = (((0, 0),), ((1, 0),), ((0, 1), (1, 1), (0, 2), (1, 2), (0, 3), (1, 3)))
REST = (False, True, True)
WEIGHTS = (0.15, 0.35, 0.15)


def dot(a, b, dims):
    return lax.dot_general(a, b, (dims, ((), ())), preferred_element_type=F32)


def normalize(raw):
    data = raw.astype(F32)
    inverse = lax.rsqrt(jnp.mean(data * data, axis=-1, keepdims=True) + EPSILON)
    return data * inverse, inverse


def norm_back(unit, inverse, gain, upstream):
    scaled = upstream * gain
    return inverse * (scaled - unit * jnp.mean(scaled * unit, axis=-1, keepdims=True))


def write_out(d_proj, d_w, d_proj_out, d_w_out):
    d_proj_out[...] = d_proj[...]
    d_w_out[...] = d_w[...]


def batch_bounds(ny, nz, parts):
    n = ny * nz
    hops = [((n - step) // ny + 1) // 2 for step in range(1, n)]
    whole, bounds, done, share = sum(hops), [1], 0, 0.0
    for part in parts[:-1]:
        share += part
        step = bounds[-1]
        while step < n and done + hops[step - 1] / 2 <= share * whole:
            done += hops[step - 1]
            step += 1
        bounds.append(step)
    return bounds + [n]


def kernel(ny, nz, gain, ids_row, proj_in, d_out_in, w_out_in, d_proj, d_w,
           proj, d_out, w_out, sent, arrived, back0, back1, back2, home0, home1, home2,
           rest, rest_a, rest_b, d_cols, d_cols_t, att, att_all, part, mine, pair_out, pair_in,
           out_r, out_l, in_r, in_l, qs, ks, vs, gs, low, grad_low,
           codes, chooser_t, in_sems, sems, ring_sems):
    n = ny * nz
    tokens = proj.shape[0]
    slots = n * CAP
    width = d_out.shape[1] // ny
    rows_z = width // nz
    me = lax.axis_index("seq")
    my_y, my_z = lax.div(me, nz), lax.rem(me, nz)

    def other(step, mirror=False):
        step = n - step
        j, dy = lax.div(step, ny), lax.rem(step, ny)
        dz = jnp.where(lax.rem(j, 2) == 1, lax.div(j + 1, 2), nz - lax.div(j, 2))
        if mirror:
            dz = jnp.where(2 * dy < ny, dz, 2 * nz - dz)
        return lax.rem(my_y + dy, ny) * nz + lax.rem(my_z + dz, nz)

    def along_y(dy):
        return lax.rem(my_y + dy, ny) * nz + my_z

    def copy_to(src, dst, send_sem, recv_sem, target):
        return pltpu.make_async_remote_copy(
            src_ref=src, dst_ref=dst, send_sem=send_sem, recv_sem=recv_sem,
            device_id={"seq": target}, device_id_type=pl.DeviceIdType.MESH)

    def remote(src, dst, number, target):
        return copy_to(src, dst, sems.at[2 * number], sems.at[2 * number + 1], target)

    def wait_for(ref, sem):
        pltpu.make_async_copy(ref, ref, sem).wait()

    def wait_sent(ref, number):
        wait_for(ref, sems.at[2 * number])

    def wait_arrived(ref, number):
        wait_for(ref, sems.at[2 * number + 1])

    loads = [pltpu.make_async_copy(src, dst, in_sems.at[i]) for i, (src, dst) in enumerate(
        ((proj_in, proj), (w_out_in, w_out), (d_out_in, d_out)))]
    for load in loads:
        load.start()
    barrier = pltpu.get_barrier_semaphore()

    @pl.loop(1, n)
    def _(step):
        pl.semaphore_signal(barrier, inc=1, device_id={"seq": other(step)},
                            device_id_type=pl.DeviceIdType.MESH)

    for load in loads:
        load.wait()

    grad_att = dot(d_out[...], w_out[...], ((1,), (0,))).astype(BF16)
    ones = jnp.ones((tokens, HS), BF16)

    def main_block(rows):
        return rows[:n * MAIN].reshape(n, MAIN, HS)

    def put_rest(ref, at, rows):
        for r in range(CAP - MAIN):
            start = n * (MAIN + r)
            ref[pl.ds(at + r, n, stride=BLOCK), :] = rows[start:start + n]

    def rest_block(ref):
        return ref[...].reshape(n, BLOCK, HS)

    def slots_of(block, ref, at):
        pieces = [block.reshape(n * MAIN, HS)]
        for r in range(CAP - MAIN):
            pieces.append(ref[pl.ds(at + r, n, stride=BLOCK), :])
        return jnp.concatenate(pieces, axis=0)

    def block_of(message, i):
        return message[:, i * BLOCK:(i + 1) * BLOCK]

    def to_all(src, dst, number, steps=(1, n), mirror=False):
        @pl.loop(*steps)
        def _(step):
            target = other(step, mirror)
            remote(src.at[target], dst.at[me], number, target).start()

    def pack(h):
        first = h * 3 * HS
        q_unit, _ = normalize(proj[:, first:first + HS])
        k_unit, _ = normalize(proj[:, first + HS:first + 2 * HS])
        payload = jnp.concatenate(
            [(q_unit * gain[0:1, :]).astype(BF16), (k_unit * gain[1:2, :]).astype(BF16),
             proj[:, first + 2 * HS:first + 3 * HS], grad_att[:, h * HS:(h + 1) * HS], ones], axis=1)
        row = ids_row[h].astype(F32)
        col = jnp.broadcast_to(row, (tokens, tokens)).T
        t0 = lax.broadcasted_iota(jnp.int32, (tokens, tokens), 0)
        t1 = lax.broadcasted_iota(jnp.int32, (tokens, tokens), 1)
        rank = jnp.sum(jnp.where((row == col) & (t0 < t1), 1.0, 0.0), axis=0, keepdims=True)
        code = jnp.where(rank < MAIN, row * MAIN + rank, n * MAIN + (rank - MAIN) * n + row)
        codes[h] = code
        chooser = jnp.where(
            code.astype(jnp.int32) == lax.broadcasted_iota(jnp.int32, (slots, tokens), 0), 1.0, 0.0).astype(BF16)
        rows = dot(chooser, payload, ((1,), (0,)))
        live = rows[:, 4 * HS:]
        parts = [rows[:, :HS], rows[:, HS:2 * HS],
                 rows[:, 2 * HS:3 * HS] + (1.0 - live) * DEAD, rows[:, 3 * HS:4 * HS]]
        for c in range(4):
            put_rest(rest, c * 2, parts[c])
        sent[h] = jnp.concatenate([main_block(p) for p in parts] + [rest_block(rest)], axis=1).astype(BF16)

    pack(0)
    pl.semaphore_wait(barrier, n - 1)
    to_all(sent.at[0], arrived.at[0], 0)
    pack(1)
    to_all(sent.at[1], arrived.at[1], 1)

    for dy in range(1, ny):
        start = pl.multiple_of(lax.rem(my_y + dy, ny) * width, width)
        remote(d_out.at[:, pl.ds(start, width)], d_cols.at[my_y], 2, along_y(dy)).start()
    own = pl.multiple_of(my_y * width, width)
    d_cols[my_y] = d_out[:, pl.ds(own, width)]
    for h in range(HEADS):
        arrived[h, me] = sent[h, me]
        code = jnp.broadcast_to(codes[h], (tokens, tokens)).T[:, 0:1].astype(jnp.int32)
        chooser_t[h] = jnp.where(
            code == lax.broadcasted_iota(jnp.int32, (tokens, slots), 1), 1.0, 0.0).astype(BF16)

    scale = HS ** -0.5

    def own_cluster(h):
        message = arrived[h].astype(F32)
        rest[...] = block_of(message, OUT_BLOCKS - 1).reshape(n * BLOCK, HS)
        for c, ref in enumerate((qs, ks, vs, gs)):
            rows = slots_of(block_of(message, c), rest, c * 2)
            if c == 2:
                live = jnp.where(rows < DEAD / 2, 1.0, 0.0)[:, 0:1]
                rows = jnp.where(rows < DEAD / 2, rows, 0.0)
            ref[...] = rows.astype(BF16)
        out_t, grad_q_t = [], []
        for start in range(0, slots, 2 * HS):
            size = min(2 * HS, slots - start)
            block = slice(start, start + size)
            scores = dot(ks[...], qs[block], ((1,), (1,))) * scale
            expo = jnp.exp(scores) * live
            total = jnp.sum(expo, axis=0, keepdims=True)
            total = jnp.where(total == 0.0, 1.0, total)
            probs = expo / total
            probs_low = probs.astype(BF16)
            grad_probs = dot(vs[...], gs[block], ((1,), (1,)))
            row_dot = jnp.sum(probs * grad_probs, axis=0, keepdims=True)
            grad_scores = (probs * (grad_probs - row_dot) * scale).astype(BF16)
            low[:, block] = probs_low
            grad_low[:, block] = grad_scores
            out_t.append(dot(vs[...], probs_low, ((0,), (0,))))
            grad_q_t.append(dot(ks[...], grad_scores, ((0,), (0,))))
        out = jnp.concatenate(out_t, axis=1).T
        grad_q = jnp.concatenate(grad_q_t, axis=1).T
        grad_k = dot(grad_low[...], qs[...], ((1,), (0,)))
        grad_v = dot(low[...], gs[...], ((1,), (0,)))
        parts = [out, grad_q, grad_k, grad_v]
        for c in range(4):
            put_rest(rest_a if c < 2 else rest_b, c % 2 * 4 + h * 2, parts[c])
        return [main_block(p) for p in parts]

    def message_back(i, results):
        blocks = [results[h][c] for h, c in BACK[i]]
        if REST[i]:
            blocks.append(rest_block(rest_a if i == 1 else rest_b))
        return jnp.concatenate(blocks, axis=1).astype(BF16)

    wait_arrived(arrived.at[0, pl.ds(0, n - 1)], 0)
    results = [own_cluster(0)]
    back0[...] = message_back(0, results)
    to_all(back0, home0, 3)
    home0[me] = back0[me]
    wait_arrived(d_cols.at[pl.ds(0, ny - 1)], 2)
    for y in range(ny):
        d_cols_t[:, y * tokens:(y + 1) * tokens] = d_cols[y].T
    wait_arrived(arrived.at[1, pl.ds(0, n - 1)], 1)
    results.append(own_cluster(1))
    back1[...] = message_back(1, results)
    to_all(back1, home1, 4)
    back2[...] = message_back(2, results)

    members = nz // 2
    half = members // 2
    bounds = batch_bounds(ny, nz, WEIGHTS + ((1 - sum(WEIGHTS)) / half,) * half)

    def send_batch(i):
        to_all(back2, home2, 5, (bounds[i], bounds[i + 1]), mirror=True)

    send_batch(0)
    home1[me] = back1[me]
    home2[me] = back2[me]

    wait_arrived(home1.at[pl.ds(0, n - 1)], 4)
    wait_arrived(home0.at[pl.ds(0, n - 1)], 3)
    first_message, message = home0[...].astype(F32), home1[...].astype(F32)
    rest_a[...] = block_of(message, 1).reshape(n * BLOCK, HS)
    for h in range(HEADS):
        block = block_of((first_message, message)[h], 0)
        rows = slots_of(block, rest_a, h * 2).astype(BF16)
        att[:, h * HS:(h + 1) * HS] = dot(chooser_t[h], rows, ((1,), (0,))).astype(BF16)
    for dy in range(1, ny):
        remote(att, att_all.at[my_y], 6, along_y(dy)).start()
    send_batch(1)
    att_all[my_y] = att[...]
    wait_arrived(att_all.at[pl.ds(0, ny - 1)], 6)
    gathered = att_all[...].reshape(ny * tokens, HEADS * HS)
    part[...] = dot(d_cols_t[...], gathered, ((1,), (0,))).reshape(members, 2, rows_z, HEADS * HS)

    odd = lax.rem(my_z, 2)
    for h in range(HEADS):
        side = 1 - 2 * odd if h == 0 else 2 * odd - 1
        partner = my_y * nz + lax.rem(my_z + side + nz, nz)
        pair_out[h] = part[:, 1 - odd, :, h * HS:(h + 1) * HS].astype(BF16)
        remote(pair_out.at[h], pair_in.at[h], 7 + h, partner).start()
    send_batch(2)
    for h in range(HEADS):
        wait_arrived(pair_in.at[h], 7 + h)
        mine[:, :, h * HS:(h + 1) * HS] = part[:, odd, :, h * HS:(h + 1) * HS] + pair_in[h].astype(F32)

    my_place = lax.div(my_z, 2)
    right = my_y * nz + lax.rem(my_z + 2, nz)
    left = my_y * nz + lax.rem(my_z + nz - 2, nz)

    def part_of(away):
        return mine[lax.rem(my_place + away, members)]

    def ring_copies(k):
        copies = [copy_to(out_r.at[k], in_r.at[k], ring_sems.at[0], ring_sems.at[2 + k], right)]
        if k < half - 1:
            copies.append(copy_to(out_l.at[k], in_l.at[k], ring_sems.at[1], ring_sems.at[2 + half + k], left))
        return copies

    for k in range(half):
        to_right, to_left = part_of(half - k), part_of(members - half + 1 + k)
        if k > 0:
            to_right = to_right + in_r[k - 1].astype(F32)
            if k < half - 1:
                to_left = to_left + in_l[k - 1].astype(F32)
        out_r[k] = to_right.astype(BF16)
        if k < half - 1:
            out_l[k] = to_left.astype(BF16)
        for copy in ring_copies(k):
            copy.start()
        send_batch(len(WEIGHTS) + k)
        for copy in ring_copies(k):
            copy.wait_recv()
    total = part_of(0) + in_r[half - 1].astype(F32) + in_l[half - 2].astype(F32)
    d_w[...] = total * (tokens * n) ** -0.5

    wait_arrived(home2.at[pl.ds(0, n - 1)], 5)
    message = home2[...].astype(F32)
    rest_b[...] = block_of(message, len(BACK[2])).reshape(n * BLOCK, HS)
    for h in range(HEADS):
        grads = []
        for c in range(1, 4):
            block = block_of(message, BACK[2].index((h, c)))
            grads.append(slots_of(block, rest_a if c < 2 else rest_b, c % 2 * 4 + h * 2).astype(BF16))
        found = dot(chooser_t[h], jnp.concatenate(grads, axis=1), ((1,), (0,)))
        first = h * 3 * HS
        for c in range(2):
            unit, inverse = normalize(proj[:, first + c * HS:first + (c + 1) * HS])
            d_proj[:, first + c * HS:first + (c + 1) * HS] = norm_back(
                unit, inverse, gain[c:c + 1, :], found[:, c * HS:(c + 1) * HS]).astype(BF16)
        d_proj[:, first + 2 * HS:first + 3 * HS] = found[:, 2 * HS:].astype(BF16)

    for h in range(HEADS):
        wait_sent(sent.at[h, pl.ds(0, n - 1)], h)
    wait_sent(d_cols.at[pl.ds(0, ny - 1)], 2)
    wait_sent(back0.at[pl.ds(0, n - 1)], 3)
    wait_sent(back1.at[pl.ds(0, n - 1)], 4)
    wait_sent(back2.at[pl.ds(0, n - 1)], 5)
    wait_sent(att_all.at[pl.ds(0, ny - 1)], 6)
    for h in range(HEADS):
        wait_sent(pair_out.at[h], 7 + h)
    wait_for(out_r, ring_sems.at[0])
    wait_for(out_l, ring_sems.at[1])


def per_device(ny, projections, qk_gain, clusters, d_out, w_out):
    tokens = projections.shape[0]
    n = lax.axis_size("seq")
    nz = n // ny
    slots = n * CAP
    width = d_out.shape[1] // ny
    columns = HEADS * HS
    vmem = pltpu.VMEM
    members = nz // 2
    half = members // 2
    rows_z = width // nz
    ring = (rows_z, columns)
    back = [vmem((n, (len(BACK[i]) + REST[i]) * BLOCK, HS), BF16) for i in range(3)]
    rest = vmem((n * BLOCK, HS), F32)
    scratch = [
        vmem(projections.shape, BF16), vmem(d_out.shape, BF16), vmem(w_out.shape, BF16),
        vmem((HEADS, n, OUT_BLOCKS * BLOCK, HS), BF16), vmem((HEADS, n, OUT_BLOCKS * BLOCK, HS), BF16),
        *back, *back, rest, rest, rest,
        vmem((ny, tokens, width), BF16), vmem((width, ny * tokens), BF16),
        vmem((tokens, columns), BF16), vmem((ny, tokens, columns), BF16),
        vmem((members, 2, *ring), F32), vmem((members, *ring), F32),
        vmem((HEADS, members, rows_z, HS), BF16), vmem((HEADS, members, rows_z, HS), BF16),
        vmem((half, *ring), BF16), vmem((half - 1, *ring), BF16),
        vmem((half, *ring), BF16), vmem((half - 1, *ring), BF16),
        vmem((slots, HS), BF16), vmem((slots, HS), BF16), vmem((slots, HS), BF16), vmem((slots, HS), BF16),
        vmem((slots, slots), BF16), vmem((slots, slots), BF16),
        vmem((HEADS, 1, tokens), F32), vmem((HEADS, tokens, slots), BF16),
        pltpu.SemaphoreType.DMA((3,)), pltpu.SemaphoreType.DMA((18,)), pltpu.SemaphoreType.DMA((2 + members - 1,)),
    ]
    whole = pl.BlockSpec(memory_space=pltpu.VMEM)
    anywhere = pl.BlockSpec(memory_space=pl.ANY)
    shapes = (jax.ShapeDtypeStruct(projections.shape, BF16),
              jax.ShapeDtypeStruct((width // nz, columns), F32))
    results = pl.pallas_call(
        functools.partial(kernel, ny, nz),
        out_shape=shapes,
        in_specs=[whole] * 2 + [anywhere] * 3,
        out_specs=(whole, whole),
        scratch_shapes=scratch,
        compiler_params=pltpu.CompilerParams(
            collective_id=0, has_side_effects=True, vmem_limit_bytes=56 * 1024 * 1024),
    )(qk_gain, clusters.reshape(HEADS, 1, tokens), projections, d_out, w_out)
    return pl.pallas_call(
        write_out, out_shape=shapes, in_specs=[whole] * 2, out_specs=(whole, whole))(*results)


def solution(mesh):
    ny = 4 if mesh.shape["seq"] == 64 else 2
    in_specs = (P("seq", "mp"), P(), P("mp", "seq", None), P("seq", None), P(None, "mp"))
    out_specs = (P("seq", "mp"), P("seq", "mp"))
    return jax.shard_map(functools.partial(per_device, ny), mesh=mesh, in_specs=in_specs,
                         out_specs=out_specs, check_vma=False)
```

```python
import functools

import jax
import jax.numpy as jnp
from jax import lax
from jax.experimental import pallas as pl
from jax.experimental.pallas import tpu as pltpu
from jax.sharding import PartitionSpec as P

EPSILON = 1e-06
HS = 128
HEADS = 2
CAP = 10
MAIN = 8
DEAD = 1024.0
F32 = jnp.float32
BF16 = jnp.bfloat16

BLOCK = 8
OUT_BLOCKS = 5
BACK = (((0, 0),), ((1, 0),), ((0, 1), (1, 1), (0, 2), (1, 2), (0, 3), (1, 3)))
REST = (False, True, True)
WEIGHTS = (0.15, 0.3, 0.12)


def dot(a, b, dims):
    return lax.dot_general(a, b, (dims, ((), ())), preferred_element_type=F32)


def normalize(raw):
    data = raw.astype(F32)
    inverse = lax.rsqrt(jnp.mean(data * data, axis=-1, keepdims=True) + EPSILON)
    return data * inverse, inverse


def norm_back(unit, inverse, gain, upstream):
    scaled = upstream * gain
    return inverse * (scaled - unit * jnp.mean(scaled * unit, axis=-1, keepdims=True))


def write_out(d_proj, d_w, d_proj_out, d_w_out):
    d_proj_out[...] = d_proj[...]
    d_w_out[...] = d_w[...]


def batch_bounds(ny, nz, parts):
    n = ny * nz
    hops = [((n - step) // ny + 1) // 2 for step in range(1, n)]
    whole, bounds, done, share = sum(hops), [1], 0, 0.0
    for part in parts[:-1]:
        share += part
        step = bounds[-1]
        while step < n and done + hops[step - 1] / 2 <= share * whole:
            done += hops[step - 1]
            step += 1
        bounds.append(step)
    return bounds + [n]


def kernel(ny, nz, gain, ids_row, proj_in, d_out_in, w_out_in, d_proj, d_w,
           proj, d_out, w_out, sent, arrived, back0, back1, back2, home0, home1, home2,
           rest, rest_a, rest_b, d_cols, d_cols_t, att, att_all, part, mine, pair_out, pair_in,
           out_r, out_l, in_r, in_l, qs, ks, vs, gs, low, grad_low,
           codes, chooser_t, in_sems, sems, ring_sems):
    n = ny * nz
    tokens = proj.shape[0]
    slots = n * CAP
    width = d_out.shape[1] // ny
    rows_z = width // nz
    me = lax.axis_index("seq")
    my_y, my_z = lax.div(me, nz), lax.rem(me, nz)

    def other(step, mirror=False):
        step = n - step
        j, dy = lax.div(step, ny), lax.rem(step, ny)
        dz = jnp.where(lax.rem(j, 2) == 1, lax.div(j + 1, 2), nz - lax.div(j, 2))
        if mirror:
            dz = jnp.where(lax.rem(dy, 2) == 0, dz, 2 * nz - dz)
        return lax.rem(my_y + dy, ny) * nz + lax.rem(my_z + dz, nz)

    def along_y(dy):
        return lax.rem(my_y + dy, ny) * nz + my_z

    def copy_to(src, dst, send_sem, recv_sem, target):
        return pltpu.make_async_remote_copy(
            src_ref=src, dst_ref=dst, send_sem=send_sem, recv_sem=recv_sem,
            device_id={"seq": target}, device_id_type=pl.DeviceIdType.MESH)

    def remote(src, dst, number, target):
        return copy_to(src, dst, sems.at[2 * number], sems.at[2 * number + 1], target)

    def wait_for(ref, sem):
        pltpu.make_async_copy(ref, ref, sem).wait()

    def wait_sent(ref, number):
        wait_for(ref, sems.at[2 * number])

    def wait_arrived(ref, number):
        wait_for(ref, sems.at[2 * number + 1])

    loads = [pltpu.make_async_copy(src, dst, in_sems.at[i]) for i, (src, dst) in enumerate(
        ((proj_in, proj), (w_out_in, w_out), (d_out_in, d_out)))]
    for load in loads:
        load.start()
    barrier = pltpu.get_barrier_semaphore()

    @pl.loop(1, n)
    def _(step):
        pl.semaphore_signal(barrier, inc=1, device_id={"seq": other(step)},
                            device_id_type=pl.DeviceIdType.MESH)

    for load in loads:
        load.wait()

    grad_att = dot(d_out[...], w_out[...], ((1,), (0,))).astype(BF16)
    ones = jnp.ones((tokens, HS), BF16)

    def main_block(rows):
        return rows[:n * MAIN].reshape(n, MAIN, HS)

    def put_rest(ref, at, rows):
        for r in range(CAP - MAIN):
            start = n * (MAIN + r)
            ref[pl.ds(at + r, n, stride=BLOCK), :] = rows[start:start + n]

    def rest_block(ref):
        return ref[...].reshape(n, BLOCK, HS)

    def slots_of(block, ref, at):
        pieces = [block.reshape(n * MAIN, HS)]
        for r in range(CAP - MAIN):
            pieces.append(ref[pl.ds(at + r, n, stride=BLOCK), :])
        return jnp.concatenate(pieces, axis=0)

    def block_of(message, i):
        return message[:, i * BLOCK:(i + 1) * BLOCK]

    def to_all(src, dst, number, steps=(1, n), mirror=True):
        @pl.loop(*steps)
        def _(step):
            target = other(step, mirror)
            remote(src.at[target], dst.at[me], number, target).start()

    def pack(h):
        first = h * 3 * HS
        q_unit, _ = normalize(proj[:, first:first + HS])
        k_unit, _ = normalize(proj[:, first + HS:first + 2 * HS])
        payload = jnp.concatenate(
            [(q_unit * gain[0:1, :]).astype(BF16), (k_unit * gain[1:2, :]).astype(BF16),
             proj[:, first + 2 * HS:first + 3 * HS], grad_att[:, h * HS:(h + 1) * HS], ones], axis=1)
        row = ids_row[h].astype(F32)
        col = jnp.broadcast_to(row, (tokens, tokens)).T
        t0 = lax.broadcasted_iota(jnp.int32, (tokens, tokens), 0)
        t1 = lax.broadcasted_iota(jnp.int32, (tokens, tokens), 1)
        rank = jnp.sum(jnp.where((row == col) & (t0 < t1), 1.0, 0.0), axis=0, keepdims=True)
        code = jnp.where(rank < MAIN, row * MAIN + rank, n * MAIN + (rank - MAIN) * n + row)
        codes[h] = code
        chooser = jnp.where(
            code.astype(jnp.int32) == lax.broadcasted_iota(jnp.int32, (slots, tokens), 0), 1.0, 0.0).astype(BF16)
        rows = dot(chooser, payload, ((1,), (0,)))
        live = rows[:, 4 * HS:]
        parts = [rows[:, :HS], rows[:, HS:2 * HS],
                 rows[:, 2 * HS:3 * HS] + (1.0 - live) * DEAD, rows[:, 3 * HS:4 * HS]]
        for c in range(4):
            put_rest(rest, c * 2, parts[c])
        sent[h] = jnp.concatenate([main_block(p) for p in parts] + [rest_block(rest)], axis=1).astype(BF16)

    pack(0)
    pl.semaphore_wait(barrier, n - 1)
    to_all(sent.at[0], arrived.at[0], 0)
    pack(1)
    to_all(sent.at[1], arrived.at[1], 1)

    for dy in range(1, ny):
        start = pl.multiple_of(lax.rem(my_y + dy, ny) * width, width)
        remote(d_out.at[:, pl.ds(start, width)], d_cols.at[my_y], 2, along_y(dy)).start()
    own = pl.multiple_of(my_y * width, width)
    d_cols[my_y] = d_out[:, pl.ds(own, width)]
    for h in range(HEADS):
        arrived[h, me] = sent[h, me]
        code = jnp.broadcast_to(codes[h], (tokens, tokens)).T[:, 0:1].astype(jnp.int32)
        chooser_t[h] = jnp.where(
            code == lax.broadcasted_iota(jnp.int32, (tokens, slots), 1), 1.0, 0.0).astype(BF16)

    scale = HS ** -0.5

    def own_cluster(h):
        message = arrived[h].astype(F32)
        rest[...] = block_of(message, OUT_BLOCKS - 1).reshape(n * BLOCK, HS)
        for c, ref in enumerate((qs, ks, vs, gs)):
            rows = slots_of(block_of(message, c), rest, c * 2)
            if c == 2:
                live = jnp.where(rows < DEAD / 2, 1.0, 0.0)[:, 0:1]
                rows = jnp.where(rows < DEAD / 2, rows, 0.0)
            ref[...] = rows.astype(BF16)
        out_t, grad_q_t = [], []
        for start in range(0, slots, 2 * HS):
            size = min(2 * HS, slots - start)
            block = slice(start, start + size)
            scores = dot(ks[...], qs[block], ((1,), (1,))) * scale
            expo = jnp.exp(scores) * live
            total = jnp.sum(expo, axis=0, keepdims=True)
            total = jnp.where(total == 0.0, 1.0, total)
            probs = expo / total
            probs_low = probs.astype(BF16)
            grad_probs = dot(vs[...], gs[block], ((1,), (1,)))
            row_dot = jnp.sum(probs * grad_probs, axis=0, keepdims=True)
            grad_scores = (probs * (grad_probs - row_dot) * scale).astype(BF16)
            low[:, block] = probs_low
            grad_low[:, block] = grad_scores
            out_t.append(dot(vs[...], probs_low, ((0,), (0,))))
            grad_q_t.append(dot(ks[...], grad_scores, ((0,), (0,))))
        out = jnp.concatenate(out_t, axis=1).T
        grad_q = jnp.concatenate(grad_q_t, axis=1).T
        grad_k = dot(grad_low[...], qs[...], ((1,), (0,)))
        grad_v = dot(low[...], gs[...], ((1,), (0,)))
        parts = [out, grad_q, grad_k, grad_v]
        for c in range(4):
            put_rest(rest_a if c < 2 else rest_b, c % 2 * 4 + h * 2, parts[c])
        return [main_block(p) for p in parts]

    def message_back(i, results):
        blocks = [results[h][c] for h, c in BACK[i]]
        if REST[i]:
            blocks.append(rest_block(rest_a if i == 1 else rest_b))
        return jnp.concatenate(blocks, axis=1).astype(BF16)

    wait_arrived(arrived.at[0, pl.ds(0, n - 1)], 0)
    results = [own_cluster(0)]
    back0[...] = message_back(0, results)
    to_all(back0, home0, 3)
    home0[me] = back0[me]
    wait_arrived(d_cols.at[pl.ds(0, ny - 1)], 2)
    for y in range(ny):
        d_cols_t[:, y * tokens:(y + 1) * tokens] = d_cols[y].T
    wait_arrived(arrived.at[1, pl.ds(0, n - 1)], 1)
    results.append(own_cluster(1))
    back1[...] = message_back(1, results)
    to_all(back1, home1, 4)
    back2[...] = message_back(2, results)

    members = nz // 2
    half = members // 2
    bounds = batch_bounds(ny, nz, WEIGHTS + ((1 - sum(WEIGHTS)) / half,) * half)

    def send_batch(i):
        to_all(back2, home2, 5, (bounds[i], bounds[i + 1]), mirror=True)

    send_batch(0)
    home1[me] = back1[me]
    home2[me] = back2[me]

    wait_arrived(home1.at[pl.ds(0, n - 1)], 4)
    wait_arrived(home0.at[pl.ds(0, n - 1)], 3)
    first_message, message = home0[...].astype(F32), home1[...].astype(F32)
    rest_a[...] = block_of(message, 1).reshape(n * BLOCK, HS)
    for h in range(HEADS):
        block = block_of((first_message, message)[h], 0)
        rows = slots_of(block, rest_a, h * 2).astype(BF16)
        att[:, h * HS:(h + 1) * HS] = dot(chooser_t[h], rows, ((1,), (0,))).astype(BF16)
    for dy in range(1, ny):
        remote(att, att_all.at[my_y], 6, along_y(dy)).start()
    send_batch(1)
    att_all[my_y] = att[...]
    wait_arrived(att_all.at[pl.ds(0, ny - 1)], 6)
    gathered = att_all[...].reshape(ny * tokens, HEADS * HS)
    part[...] = dot(d_cols_t[...], gathered, ((1,), (0,))).reshape(members, 2, rows_z, HEADS * HS)

    odd = lax.rem(my_z, 2)
    for h in range(HEADS):
        side = 1 - 2 * odd if h == 0 else 2 * odd - 1
        partner = my_y * nz + lax.rem(my_z + side + nz, nz)
        pair_out[h] = part[:, 1 - odd, :, h * HS:(h + 1) * HS].astype(BF16)
        remote(pair_out.at[h], pair_in.at[h], 7 + h, partner).start()
    send_batch(2)
    for h in range(HEADS):
        wait_arrived(pair_in.at[h], 7 + h)
        mine[:, :, h * HS:(h + 1) * HS] = part[:, odd, :, h * HS:(h + 1) * HS] + pair_in[h].astype(F32)

    my_place = lax.div(my_z, 2)
    right = my_y * nz + lax.rem(my_z + 2, nz)
    left = my_y * nz + lax.rem(my_z + nz - 2, nz)

    def part_of(away):
        return mine[lax.rem(my_place + away, members)]

    def ring_copies(k):
        copies = [copy_to(out_r.at[k], in_r.at[k], ring_sems.at[0], ring_sems.at[2 + k], right)]
        if k < half - 1:
            copies.append(copy_to(out_l.at[k], in_l.at[k], ring_sems.at[1], ring_sems.at[2 + half + k], left))
        return copies

    for k in range(half):
        to_right, to_left = part_of(half - k), part_of(members - half + 1 + k)
        if k > 0:
            to_right = to_right + in_r[k - 1].astype(F32)
            if k < half - 1:
                to_left = to_left + in_l[k - 1].astype(F32)
        out_r[k] = to_right.astype(BF16)
        if k < half - 1:
            out_l[k] = to_left.astype(BF16)
        for copy in ring_copies(k):
            copy.start()
        send_batch(len(WEIGHTS) + k)
        for copy in ring_copies(k):
            copy.wait_recv()
    total = part_of(0) + in_r[half - 1].astype(F32) + in_l[half - 2].astype(F32)
    d_w[...] = total * (tokens * n) ** -0.5

    wait_arrived(home2.at[pl.ds(0, n - 1)], 5)
    message = home2[...].astype(F32)
    rest_b[...] = block_of(message, len(BACK[2])).reshape(n * BLOCK, HS)
    for h in range(HEADS):
        grads = []
        for c in range(1, 4):
            block = block_of(message, BACK[2].index((h, c)))
            grads.append(slots_of(block, rest_a if c < 2 else rest_b, c % 2 * 4 + h * 2).astype(BF16))
        found = dot(chooser_t[h], jnp.concatenate(grads, axis=1), ((1,), (0,)))
        first = h * 3 * HS
        for c in range(2):
            unit, inverse = normalize(proj[:, first + c * HS:first + (c + 1) * HS])
            d_proj[:, first + c * HS:first + (c + 1) * HS] = norm_back(
                unit, inverse, gain[c:c + 1, :], found[:, c * HS:(c + 1) * HS]).astype(BF16)
        d_proj[:, first + 2 * HS:first + 3 * HS] = found[:, 2 * HS:].astype(BF16)

    for h in range(HEADS):
        wait_sent(sent.at[h, pl.ds(0, n - 1)], h)
    wait_sent(d_cols.at[pl.ds(0, ny - 1)], 2)
    wait_sent(back0.at[pl.ds(0, n - 1)], 3)
    wait_sent(back1.at[pl.ds(0, n - 1)], 4)
    wait_sent(back2.at[pl.ds(0, n - 1)], 5)
    wait_sent(att_all.at[pl.ds(0, ny - 1)], 6)
    for h in range(HEADS):
        wait_sent(pair_out.at[h], 7 + h)
    wait_for(out_r, ring_sems.at[0])
    wait_for(out_l, ring_sems.at[1])


def per_device(ny, projections, qk_gain, clusters, d_out, w_out):
    tokens = projections.shape[0]
    n = lax.axis_size("seq")
    nz = n // ny
    slots = n * CAP
    width = d_out.shape[1] // ny
    columns = HEADS * HS
    vmem = pltpu.VMEM
    members = nz // 2
    half = members // 2
    rows_z = width // nz
    ring = (rows_z, columns)
    back = [vmem((n, (len(BACK[i]) + REST[i]) * BLOCK, HS), BF16) for i in range(3)]
    rest = vmem((n * BLOCK, HS), F32)
    scratch = [
        vmem(projections.shape, BF16), vmem(d_out.shape, BF16), vmem(w_out.shape, BF16),
        vmem((HEADS, n, OUT_BLOCKS * BLOCK, HS), BF16), vmem((HEADS, n, OUT_BLOCKS * BLOCK, HS), BF16),
        *back, *back, rest, rest, rest,
        vmem((ny, tokens, width), BF16), vmem((width, ny * tokens), BF16),
        vmem((tokens, columns), BF16), vmem((ny, tokens, columns), BF16),
        vmem((members, 2, *ring), F32), vmem((members, *ring), F32),
        vmem((HEADS, members, rows_z, HS), BF16), vmem((HEADS, members, rows_z, HS), BF16),
        vmem((half, *ring), BF16), vmem((half - 1, *ring), BF16),
        vmem((half, *ring), BF16), vmem((half - 1, *ring), BF16),
        vmem((slots, HS), BF16), vmem((slots, HS), BF16), vmem((slots, HS), BF16), vmem((slots, HS), BF16),
        vmem((slots, slots), BF16), vmem((slots, slots), BF16),
        vmem((HEADS, 1, tokens), F32), vmem((HEADS, tokens, slots), BF16),
        pltpu.SemaphoreType.DMA((3,)), pltpu.SemaphoreType.DMA((18,)), pltpu.SemaphoreType.DMA((2 + members - 1,)),
    ]
    whole = pl.BlockSpec(memory_space=pltpu.VMEM)
    anywhere = pl.BlockSpec(memory_space=pl.ANY)
    shapes = (jax.ShapeDtypeStruct(projections.shape, BF16),
              jax.ShapeDtypeStruct((width // nz, columns), F32))
    results = pl.pallas_call(
        functools.partial(kernel, ny, nz),
        out_shape=shapes,
        in_specs=[whole] * 2 + [anywhere] * 3,
        out_specs=(whole, whole),
        scratch_shapes=scratch,
        compiler_params=pltpu.CompilerParams(
            collective_id=0, has_side_effects=True, vmem_limit_bytes=56 * 1024 * 1024),
    )(qk_gain, clusters.reshape(HEADS, 1, tokens), projections, d_out, w_out)
    return pl.pallas_call(
        write_out, out_shape=shapes, in_specs=[whole] * 2, out_specs=(whole, whole))(*results)


def solution(mesh):
    ny = 4 if mesh.shape["seq"] == 64 else 2
    in_specs = (P("seq", "mp"), P(), P("mp", "seq", None), P("seq", None), P(None, "mp"))
    out_specs = (P("seq", "mp"), P("seq", "mp"))
    return jax.shard_map(functools.partial(per_device, ny), mesh=mesh, in_specs=in_specs,
                         out_specs=out_specs, check_vma=False)
```
